128 devices in a mesh: lat: 8 (over y, core), lon: 16 (over x, z).
Axes of the slice: x: 4, y: 4, z: 4, core: 2. Of those that a mesh axis runs over, the one named last changes fastest.
Arguments:
- probes: bfloat16 [8, 8, 512, 4096], P(None, None, 'lat', 'lon'), may hold values from -12 to 12
- kappa_sq: float32 [8, 512, 4096], P(None, 'lat', 'lon'), may hold values from 0.2 to 1
- cond_lat: float32 [512, 4096], P('lat', 'lon'), may hold values from 0.05 to 0.5
- cond_lon: float32 [512, 4096], P('lat', 'lon'), may hold values from 0.05 to 0.5
- innovations: float32 [8, 1048576], P(None, ('lat', 'lon')), may hold values from -6 to 6
- obs_weight: float32 [1048576], P(('lat', 'lon')), may hold values from 0.25 to 4
- station_dest: int32 [1048576, 1], P(('lat', 'lon')), may hold values from 0 to 127; in each aligned block of 8192 rows (0 to 8191, 8192 to 16383, ...) at most 128 rows name the same one
- station_cell: int32 [1048576], P(('lat', 'lon')), may hold values from 0 to 16383
Outputs:
- solution: float32 [9, 8, 512, 4096], P(None, None, 'lat', 'lon')
The draws below stay inside these ranges and needn't reach their ends.
Inputs may be any that keep to these rules, and one draw needn't show every extreme that they name: `station_dest`: among the stations of one device, at most 128 share a destination. `station_cell`: cells are numbered row by row within the destination's block of 64 x 256.
All inputs are finite; a program needn't handle non-finite values.
Results may differ from the reference program's by a relative error of at most 0.0003.
Values sent between devices are 32-bit elements; how exact they have to be, the bound alone decides.
A program may use at most 128 MiB of HBM per device.

```python
import math
import jax
import jax.numpy as jnp
import numpy as np
from jax import lax

CLAT = 64
CLON = 256
LEVELS = 8
PROBES = 8
ITERS = 2
ST_DEV = 8192
CAP = 128
STATIONS = 1048576
NLAT = 512
NLON = 4096
N_LON = 16
DEVICES = 128


def draw_probes(key, part):
    key = jax.random.fold_in(key, 11)
    main_key = jax.random.fold_in(key, 1)
    sign_key = jax.random.fold_in(key, 2)
    shape = (PROBES, LEVELS, NLAT, NLON)
    rows = jnp.exp(math.log(3.0) * jnp.arange(NLAT, dtype=jnp.float32) / max(NLAT - 1, 1))[:, None]
    signs = (2 * jax.random.randint(sign_key, (PROBES, LEVELS, 1, 1), 0, 2) - 1).astype(jnp.float32)
    base = jnp.clip(jax.random.normal(main_key, shape, jnp.float32), -3.0, 3.0)
    values = (base + signs) * rows
    return values.astype(jnp.bfloat16)


def plant(array, own_key, least, largest):
    shape = array.shape
    index_at = [jax.random.randint(jax.random.fold_in(own_key, axis), (), 0, shape[axis]) for axis in range(len(shape))]
    array = array.at[tuple(index_at)].set(least)
    longest = shape.index(max(shape))
    index_at[longest] = (index_at[longest] + 1) % shape[longest]
    return array.at[tuple(index_at)].set(largest)


def shard_levels(own_key, dims, split, smallest, top_value):
    level, own = 1.0, jax.random.fold_in(own_key, 6)
    for dim, parts in split:
        heights = jnp.exp(jax.random.uniform(jax.random.fold_in(own, dim), (parts,), jnp.float32, smallest / len(split), top_value / len(split)))
        level = level * jnp.repeat(heights, dims[dim] // parts).reshape([-1 if axis == dim else 1 for axis in range(len(dims))])
    return level


def routed_block(rng, own, number, rows, amount, top, most, lean):
    order = jax.random.permutation(rng, amount)
    packed, usual = shares(amount, rows * top, most, lean, True), shares(amount, rows * top, most, lean, False)
    places = jnp.arange(amount)

    def named(tallies, rotation):
        used = int((tallies > 0).sum())
        fixed = max(1, used // 4)
        moved = fixed + (places - fixed + rotation * (used - fixed)) % max(1, amount - fixed)
        return jnp.zeros((amount,), jnp.int32).at[order[jnp.where(places < fixed, places, moved)]].set(jnp.asarray(tallies, jnp.int32))

    tallies = jnp.where(number % 4 == 0, named(packed, number // 4), named(usual, number - number // 4 - 1))
    mixed = jax.random.permutation(jax.random.fold_in(own, 3), amount)
    giver, sink = mixed[0:amount // 2 * 2:2], mixed[1:amount // 2 * 2:2]
    slack = jnp.minimum(tallies[giver] - 1, most - tallies[sink]) // 2
    slack = jnp.where((giver == order[0]) | (sink == order[0]) | (tallies[sink] == 0), 0, jnp.maximum(slack, 0))
    moved = jax.random.randint(jax.random.fold_in(own, 4), (amount // 2,), 0, 1 << 20) % (slack + 1)
    tallies = tallies.at[giver].add(-moved).at[sink].add(moved)
    labels = jnp.searchsorted(jnp.cumsum(tallies), jnp.arange(rows * top), side="right").astype(jnp.int32)
    table = labels.reshape(top, rows).T
    table = table[jax.random.permutation(jax.random.fold_in(own, 1), rows)]
    rotation = jax.random.randint(jax.random.fold_in(own, 2), (rows, 1), 0, top)
    return jnp.take_along_axis(table, (jnp.arange(top)[None, :] + rotation) % top, axis=1)


def shares(amount, total, reach, skew, full):
    portions = [(1 << 20) // math.isqrt(rank ** skew) + 1 for rank in range(1, amount + 1)]
    largest = reach if full else min(reach, max(-(-total // amount), total * portions[0] // sum(portions)))
    least = 1 if total - largest >= amount - 1 else 0
    given, spare = [largest] + [least] * (amount - 1), total - largest - least * (amount - 1)
    while spare > 0:
        candidates = [i for i in range(1, amount) if given[i] < largest] or [i for i in range(1, amount) if given[i] < reach]
        pool, left = sum([portions[i] for i in candidates]), spare
        for i in candidates:
            more = min(reach - given[i], max(1, left * portions[i] // pool), spare)
            given[i] = given[i] + more
            spare = spare - more
    return np.array(given)


def centred(stream_key, shape, deviation, bound, split=(), kind=jnp.bfloat16):
    factor_of = shard_levels(stream_key, shape, split, -0.22, 0.18) if split else 1.0
    entries = jax.random.normal(stream_key, shape, jnp.float32) * deviation * factor_of
    return jnp.minimum(jnp.maximum(entries, -bound), bound).astype(kind)


def setup_inputs(seed: int = 0) -> dict:
    arg_keys = jax.random.split(jax.random.key(seed), 9)
    probes = draw_probes(jax.random.fold_in(arg_keys[8], 71), 0)
    kappa_sq = jnp.clip(jnp.exp(math.log(1.0) - 1.609438 * jax.random.uniform(arg_keys[1], (LEVELS, NLAT, NLON), jnp.float32) ** shard_levels(arg_keys[1], (LEVELS, NLAT, NLON), ((1, 8), (2, 16)), -0.2, 0.2)), 0.2, 1.0)
    cond_lat = jnp.clip(jnp.exp(math.log(0.5) - 2.3025851 * jax.random.uniform(arg_keys[2], (NLAT, NLON), jnp.float32) ** shard_levels(arg_keys[2], (NLAT, NLON), ((0, 8), (1, 16)), -0.2, 0.2)), 0.05, 0.5)
    cond_lon = jnp.clip(jnp.exp(math.log(0.5) - 2.3025851 * jax.random.uniform(arg_keys[3], (NLAT, NLON), jnp.float32) ** shard_levels(arg_keys[3], (NLAT, NLON), ((0, 8), (1, 16)), -0.2, 0.2)), 0.05, 0.5)
    innovations = centred(arg_keys[4], (LEVELS, STATIONS), 1.0, 6.0, ((1, 128),), jnp.float32)
    obs_weight = jnp.clip(jnp.exp(math.log(4.0) - 2.7725887 * jax.random.uniform(arg_keys[5], (STATIONS,), jnp.float32) ** shard_levels(arg_keys[5], (STATIONS,), ((0, 128),), -0.2, 0.2)), 0.25, 4.0)
    station_dest_keys = jax.random.split(jax.random.fold_in(arg_keys[6], 1), STATIONS // ST_DEV)
    station_dest_turns = jax.random.permutation(jax.random.fold_in(arg_keys[6], 3), STATIONS // ST_DEV)
    station_dest = jax.vmap(lambda own, number: routed_block(jax.random.fold_in(arg_keys[6], 2), own, number, ST_DEV, DEVICES, 1, CAP, 2))(station_dest_keys, station_dest_turns).reshape((STATIONS, 1))
    station_cell = plant(jax.random.randint(arg_keys[7], (STATIONS,), 0, CLAT * CLON), jax.random.fold_in(arg_keys[7], 1), 0, (CLAT * CLON) - 1).astype(jnp.int32)
    return dict(probes=probes, kappa_sq=kappa_sq, cond_lat=cond_lat, cond_lon=cond_lon, innovations=innovations, obs_weight=obs_weight, station_dest=station_dest, station_cell=station_cell)


def build_faces(cond_lat, cond_lon):
    rows = jnp.arange(NLAT, dtype=jnp.int32)[:, None]
    south = jnp.where(rows < NLAT - 1, cond_lat, jnp.zeros_like(cond_lat))
    north = jnp.concatenate([jnp.zeros((1, NLON), cond_lat.dtype), south[:-1]], 0)
    west = jnp.roll(cond_lon, 1, axis=1)
    return north, south, west, cond_lon


def operate(field, diag, north, south, west, east):
    upper = jnp.concatenate([jnp.zeros_like(field[:, :1]), field[:, :-1]], 1)
    lower = jnp.concatenate([field[:, 1:], jnp.zeros_like(field[:, :1])], 1)
    left = jnp.roll(field, 1, axis=2)
    right = jnp.roll(field, -1, axis=2)
    return diag * field - north * upper - south * lower - west * left - east * right


def reference(probes, kappa_sq, cond_lat, cond_lon, innovations, obs_weight, station_dest, station_cell):
    dest = station_dest[:, 0]
    row_glob = (dest // N_LON) * CLAT + station_cell // CLON
    col_glob = (dest % N_LON) * CLON + station_cell % CLON
    flat = (row_glob * NLON + col_glob).astype(jnp.int32)
    weighted = innovations * obs_weight[None, :]
    summed = jax.ops.segment_sum(weighted.T, flat, num_segments=NLAT * NLON)
    adjoint = summed.T.reshape(LEVELS, NLAT, NLON)
    rhs = jnp.concatenate([probes.astype(jnp.float32), adjoint[None]], 0)
    north, south, west, east = build_faces(cond_lat, cond_lon)
    diag = kappa_sq + north + south + west + east

    def apply_k(field):
        return operate(field, diag, north, south, west, east)

    def total(field):
        return jnp.sum(field, axis=(1, 2))[:, None, None]

    def solve(right):
        estimate = jnp.zeros_like(right)
        resid = right
        direction = right
        norm_now = total(resid * resid)
        for step in range(ITERS):
            kdir = apply_k(direction)
            image = apply_k(kdir)
            alpha = norm_now / total(kdir * kdir)
            estimate = estimate + alpha * direction
            resid = resid - alpha * image
            if step + 1 < ITERS:
                norm_next = total(resid * resid)
                direction = resid + (norm_next / norm_now) * direction
                norm_now = norm_next
        return estimate

    return lax.map(solve, rhs)
```

```python
import functools

import jax
import jax.numpy as jnp
from jax import lax
from jax.experimental import pallas as pl
from jax.experimental.pallas import tpu as pltpu
from jax.sharding import PartitionSpec as P

f32, bf16, i32 = jnp.float32, jnp.bfloat16, jnp.int32
MESH = pl.DeviceIdType.MESH
LAT, LON, DEV = 8, 16, 128
LEVELS, ROWS, COLS = 8, 64, 256
NP, NA, NF = 64, 8, 72
PAD = ROWS + 16
HELD, SLOTS = 8192, 128
NT = (((1,), (1,)), ((), ()))
STEP_MIN, STEP_MAX = 1.0 / 25.0, 1.0 / 0.04


def iota(shape, dim):
    return lax.broadcasted_iota(i32, shape, dim)


def split2(v):
    hi = v.astype(bf16)
    return hi, (v - hi.astype(f32)).astype(bf16)


def one_hot(mask):
    return jnp.where(mask, 1.0, 0.0).astype(bf16)


def flat_rows(block, count):
    return jnp.concatenate([block[i : i + 1] for i in range(count)], 1)


def rank_phase(dest, pos, carry, span=256):
    upper = one_hot(iota((span, span), 0) < iota((span, span), 1))
    carry[...] = jnp.zeros((DEV, 128), f32)

    def body(c, _):
        s0 = pl.multiple_of(c * span, span)
        mask = iota((DEV, span), 0) == dest[:, pl.ds(s0, span)]
        hot = jnp.where(mask, 1.0, 0.0)
        within = jnp.dot(hot.astype(bf16), upper, preferred_element_type=f32)
        before = jnp.concatenate([carry[...]] * (span // 128), 1)
        pos[:, pl.ds(s0, span)] = jnp.sum(jnp.where(mask, within + before, 0.0), axis=0, keepdims=True)
        carry[...] += jnp.sum(hot, axis=1, keepdims=True)
        return 0

    lax.fori_loop(0, HELD // span, body, 0, unroll=4)


def pack_phase(inno, weight, dest, cell, pos, acc, send, span=1024):
    acc[...] = jnp.zeros((576, 256), f32)
    part = span // 128

    def body(c, _):
        s0 = pl.multiple_of(c * span, span)
        r0 = pl.multiple_of(c * part, part)
        d = dest[:, pl.ds(s0, span)]
        d_hi = jnp.where(d >= 64, 1, 0)
        d_lo = d - d_hi * 64
        slot = pos[:, pl.ds(s0, span)].astype(i32) + d_hi * SLOTS
        hi, lo = split2(inno[:, pl.ds(s0, span)] * flat_rows(weight[pl.ds(r0, part), :], part))
        cells = flat_rows(cell[pl.ds(r0, part), :], part)
        c_row = cells // COLS
        cell_hi = (c_row * COLS).astype(f32).astype(bf16)
        cell_lo = (cells - c_row * COLS).astype(f32).astype(bf16)
        slot_hot = one_hot(iota((256, span), 0) == slot)
        hi2, lo2 = jnp.concatenate([hi, hi], 0), jnp.concatenate([lo, lo], 0)
        pair = iota((16, span), 0) // 8
        left_hi, left_lo = [], []
        for t in range(32):
            mine = one_hot((pair + 2 * t) == d_lo)
            left_hi.append(mine * hi2)
            left_lo.append(mine * lo2)
        mine = one_hot(iota((64, span), 0) == d_lo)
        left_hi.append(mine * cell_hi)
        left_lo.append(mine * cell_lo)
        acc[...] += lax.dot_general(
            jnp.concatenate(left_hi, 0), slot_hot, NT, preferred_element_type=f32
        ) + lax.dot_general(jnp.concatenate(left_lo, 0), slot_hot, NT, preferred_element_type=f32)
        return 0

    lax.fori_loop(0, HELD // span, body, 0)
    for d in range(DEV):
        lo_d, hi_d = d % 64, d // 64
        at = slice(hi_d * SLOTS, (hi_d + 1) * SLOTS)
        send[d, 0:8, :] = acc[lo_d * 8 : lo_d * 8 + 8, at]
        send[d, 8:9, :] = acc[512 + lo_d : 513 + lo_d, at]


def scatter_phase(got, adj, group=8):
    adj[...] = jnp.zeros((LEVELS * ROWS, COLS), f32)
    span = group * SLOTS

    def body(g, _):
        g0 = g * group
        cells = jnp.concatenate([got[g0 + i, 8:9, :] for i in range(group)], 1).astype(i32)
        vals = jnp.concatenate([got[g0 + i, 0:8, :] for i in range(group)], 1)
        row = cells // COLS
        col_hot = one_hot(iota((COLS, span), 0) == cells - row * COLS)
        row_hot = one_hot(iota((ROWS, span), 0) == row)
        hi, lo = split2(vals)
        left_hi = jnp.concatenate([row_hot * hi[l : l + 1] for l in range(LEVELS)], 0)
        left_lo = jnp.concatenate([row_hot * lo[l : l + 1] for l in range(LEVELS)], 0)
        adj[...] += lax.dot_general(left_hi, col_hot, NT, preferred_element_type=f32) + lax.dot_general(
            left_lo, col_hot, NT, preferred_element_type=f32
        )
        return 0

    lax.fori_loop(0, DEV // group, body, 0)


def strip_sum(sq):
    return sq[:, :128] + sq[:, 128:]


def k_pass(src, dst, first, systems, halo_l, halo_r, cols_out, kd, cf, sums, which, own=None):
    def strip(i, _):
        r0 = pl.multiple_of(i * 8, 8)
        mid, below, above = (pl.multiple_of(r0 + k, 8) for k in (8, 16, 0))
        rows8, lane, row8 = iota((8, 256), 0), iota((8, 128), 1), None
        north, south, west, east = [cf[k, pl.ds(r0, 8), :] for k in range(4)]
        hl, hr = halo_l[pl.ds(r0, 8), :], halo_r[pl.ds(r0, 8), :]
        edge_l = edge_r = jnp.zeros((8, 128), f32)
        for l in range(LEVELS):
            diag = kd[l, pl.ds(r0, 8), :]
            for s in range(systems):
                j = s * LEVELS + l
                f = first + j
                c = src[f, pl.ds(mid, 8), :]
                up = pltpu.roll(jnp.where(rows8 == 7, src[f, pl.ds(above, 8), :], c), 1, 0)
                down = pltpu.roll(jnp.where(rows8 == 0, src[f, pl.ds(below, 8), :], c), 7, 0)
                cl, cr = c[:, :128], c[:, 128:]
                left = jnp.concatenate(
                    [
                        pltpu.roll(jnp.where(lane == 127, pltpu.roll(hl, 127 - j, 1), cl), 1, 1),
                        pltpu.roll(jnp.where(lane == 127, cl, cr), 1, 1),
                    ],
                    1,
                )
                right = jnp.concatenate(
                    [
                        pltpu.roll(jnp.where(lane == 0, cr, cl), 127, 1),
                        pltpu.roll(jnp.where(lane == 0, pltpu.roll(hr, (128 - j) % 128, 1), cr), 127, 1),
                    ],
                    1,
                )
                out = diag * c - north * up - south * down - west * left - east * right
                sums[which, f] += strip_sum(out * out)
                if own is not None:
                    sums[own, f] += strip_sum(c * c)
                if dst is not None:
                    dst[f, pl.ds(mid, 8), :] = out
                if cols_out is not None:
                    edge_l = jnp.where(lane == j, pltpu.roll(out[:, :128], j, 1), edge_l)
                    edge_r = jnp.where(lane == j, pltpu.roll(out[:, 128:], j + 1, 1), edge_r)
        if cols_out is not None:
            cols_out[0, pl.ds(r0, 8), :] = edge_r
            cols_out[1, pl.ds(r0, 8), :] = edge_l
        return 0

    lax.fori_loop(0, ROWS // 8, strip, 0)


def edges_of(field, first, count, rows_out, cols_out):
    def strip(i, _):
        r0 = pl.multiple_of(i * 8, 8)
        mid = pl.multiple_of(r0 + 8, 8)
        lane = iota((8, 128), 1)
        edge_l = edge_r = jnp.zeros((8, 128), f32)
        for j in range(count):
            c = field[first + j, pl.ds(mid, 8), :]
            edge_l = jnp.where(lane == j, pltpu.roll(c[:, :128], j, 1), edge_l)
            edge_r = jnp.where(lane == j, pltpu.roll(c[:, 128:], j + 1, 1), edge_r)
        cols_out[0, pl.ds(r0, 8), :] = edge_r
        cols_out[1, pl.ds(r0, 8), :] = edge_l
        return 0

    lax.fori_loop(0, ROWS // 8, strip, 0)
    rows_of(field, first, count, rows_out)


def rows_of(field, first, count, rows_out):
    for j in range(count):
        rows_out[0, j : j + 1, :] = field[first + j, ROWS + 7 : ROWS + 8, :]
        rows_out[1, j : j + 1, :] = field[first + j, 8:9, :]


def place_rows(field, first, count, rows_in):
    for j in range(count):
        field[first + j, 7:8, :] = rows_in[0, j : j + 1, :]
        field[first + j, ROWS + 8 : ROWS + 9, :] = rows_in[1, j : j + 1, :]


def lane_totals(sums, which, first, count):
    part = jnp.sum(sums[which, first : first + count], axis=1)
    total = jnp.sum(part, axis=1, keepdims=True)
    return jnp.sum(jnp.where(iota((count, 128), 1) == iota((count, 128), 0), total, 0.0), axis=0, keepdims=True)


def main_kernel(
    probes, kappa, cond_lat, cond_lon, inno, weight, dest, cell,
    image_out, adj_out, scale_out,
    v0, v1, v2, adj, acc, pos, carry, send, got, kd, cf, sums,
    prow_s, prow_r, pcol_s, pcol_r, arow_s, arow_r, acol_s, acol_r, ptot, atot,
    ready, a2a_s, a2a_r, px_s, px_r, ax_s, ax_r, pt_s, pt_r, at_s, at_r, out_sem,
):
    la, lo = lax.axis_index("lat"), lax.axis_index("lon")
    me = la * LON + lo
    lat_peers = [(lax.rem(la + i, LAT), lo) for i in range(1, LAT)]
    lon_peers = [(la, lax.rem(lo + i, LON)) for i in range(1, LON)]
    barrier = pltpu.get_barrier_semaphore()
    for peer in lat_peers + lon_peers:
        pl.semaphore_signal(barrier, inc=1, device_id=peer, device_id_type=MESH)

    beside = [lat_peers[0], lat_peers[-1], lon_peers[0], lon_peers[-1]]

    def exchange(rows_s, rows_r, cols_s, cols_r, s_sem, r_sem, k):
        parts = [(rows_s, rows_r, 0), (rows_s, rows_r, 1), (cols_s, cols_r, 0), (cols_s, cols_r, 1)]
        copies = []
        for n, (src, dst, side) in enumerate(parts):
            copies.append(
                pltpu.make_async_remote_copy(
                    src_ref=src.at[k, side], dst_ref=dst.at[k, side], send_sem=s_sem.at[k, n],
                    recv_sem=r_sem.at[k, n], device_id=beside[n], device_id_type=MESH,
                )
            )
            copies[-1].start()
        return copies

    def wait_all(copies):
        for copy in copies:
            copy.wait()

    def to_all(make):
        def start(i, _):
            make(lax.rem(me + i, DEV)).start()
            return 0

        def wait_sent(i, _):
            make(lax.rem(me + i, DEV)).wait_send()
            return 0

        def wait_got(i, _):
            make(lax.rem(me + i, DEV)).wait_recv()
            return 0

        lax.fori_loop(1, DEV, start, 0)
        return (lambda: lax.fori_loop(1, DEV, wait_sent, 0)), (lambda: lax.fori_loop(1, DEV, wait_got, 0))

    def broadcast(buf, s_sem, r_sem):
        def make(d):
            return pltpu.make_async_remote_copy(
                src_ref=buf.at[me], dst_ref=buf.at[me], send_sem=s_sem.at[d], recv_sem=r_sem.at[me],
                device_id=(d // LON, lax.rem(d, LON)), device_id_type=MESH,
            )

        def made(d):
            return pltpu.make_async_remote_copy(
                src_ref=buf.at[d], dst_ref=buf.at[d], send_sem=s_sem.at[d], recv_sem=r_sem.at[d],
                device_id=(d // LON, lax.rem(d, LON)), device_id_type=MESH,
            )

        return make, made

    sums[...] = jnp.zeros(sums.shape, f32)
    for j in range(NP):
        v0[j, 8 : 8 + ROWS, :] = probes[j].astype(f32)
    edges_of(v0, 0, NP, prow_s.at[0], pcol_s.at[0])
    prow_s[0, 0, NP : NP + 1, :] = cond_lat[ROWS - 1 : ROWS, :]
    lane = iota((ROWS, 128), 1)
    pcol_s[0, 0] = jnp.where(lane == NP, pltpu.roll(cond_lon[:, 128:], NP + 1, 1), pcol_s[0, 0])
    pl.semaphore_wait(barrier, LAT + LON - 2)
    for peer in lon_peers:
        pl.semaphore_signal(ready, inc=1, device_id=peer, device_id_type=MESH)
    copies = exchange(prow_s, prow_r, pcol_s, pcol_r, px_s, px_r, 0)

    rank_phase(dest, pos, carry)
    pack_phase(inno, weight, dest, cell, pos, acc, send)
    pl.semaphore_wait(ready, LON - 1)

    def station_copy(d):
        return pltpu.make_async_remote_copy(
            src_ref=send.at[d], dst_ref=got.at[me], send_sem=a2a_s.at[d], recv_sem=a2a_r.at[me],
            device_id=(d // LON, lax.rem(d, LON)), device_id_type=MESH,
        )

    def station_here(d):
        return pltpu.make_async_remote_copy(
            src_ref=send.at[d], dst_ref=got.at[d], send_sem=a2a_s.at[d], recv_sem=a2a_r.at[d],
            device_id=(d // LON, lax.rem(d, LON)), device_id_type=MESH,
        )

    def send_all(make):
        def start(i, _):
            make(lax.rem(me + i, DEV)).start()
            return 0

        lax.fori_loop(1, DEV, start, 0)

    def wait_for(made):
        def wait(i, _):
            made(lax.rem(me + i, DEV)).wait()
            return 0

        lax.fori_loop(1, DEV, wait, 0)

    send_all(station_copy)
    got[me] = send[me]

    wait_all(copies)
    row0 = iota((8, 256), 0) == 0
    inner = jnp.where(row0, 0.0, 1.0)
    lat_row = iota((ROWS, COLS), 0)
    south = jnp.where((lat_row == ROWS - 1) & (la == LAT - 1), 0.0, cond_lat[...])
    cf[1] = south
    up_row = jnp.where(la == 0, 0.0, prow_r[0, 0, NP : NP + 1, :])
    cf[0] = jnp.where(lat_row == 0, up_row, pltpu.roll(cond_lat[...], 1, 0))
    west_in = pltpu.roll(pcol_r[0, 0], 128 - NP, 1)
    el, er = cond_lon[:, :128], cond_lon[:, 128:]
    cf[2, :, :128] = jnp.where(lane == 0, west_in, pltpu.roll(el, 1, 1))
    cf[2, :, 128:] = pltpu.roll(jnp.where(lane == 127, el, er), 1, 1)
    cf[3] = cond_lon[...]
    for l in range(LEVELS):
        kd[l] = kappa[l] + cf[0] + cf[1] + cf[2] + cf[3]
    place_rows(v0, 0, NP, prow_r.at[0])
    k_pass(v0, v1, 0, 8, pcol_r.at[0, 0], pcol_r.at[0, 1], pcol_s.at[1], kd, cf, sums, 1, own=0)
    rows_of(v1, 0, NP, prow_s.at[1])
    copies = exchange(prow_s, prow_r, pcol_s, pcol_r, px_s, px_r, 1)
    wait_all(copies)
    place_rows(v1, 0, NP, prow_r.at[1])
    k_pass(v1, v2, 0, 8, pcol_r.at[1, 0], pcol_r.at[1, 1], pcol_s.at[2], kd, cf, sums, 2)
    rows_of(v2, 0, NP, prow_s.at[2])
    probe_copies = exchange(prow_s, prow_r, pcol_s, pcol_r, px_s, px_r, 2)
    probe_out = pltpu.make_async_copy(
        v2.at[pl.ds(0, NP), pl.ds(8, ROWS), :], image_out.at[pl.ds(0, NP)], out_sem.at[0]
    )
    probe_out.start()

    wait_for(station_here)
    scatter_phase(got, adj)
    for l in range(LEVELS):
        v0[NP + l, 8 : 8 + ROWS, :] = adj[l * ROWS : (l + 1) * ROWS, :]
    adj_copy = pltpu.make_async_copy(v0.at[pl.ds(NP, NA), pl.ds(8, ROWS), :], adj_out, out_sem.at[1])
    adj_copy.start()
    edges_of(v0, NP, NA, arow_s.at[0], acol_s.at[0])
    copies = exchange(arow_s, arow_r, acol_s, acol_r, ax_s, ax_r, 0)

    wait_all(probe_copies)
    place_rows(v2, 0, NP, prow_r.at[2])
    k_pass(v2, None, 0, 8, pcol_r.at[2, 0], pcol_r.at[2, 1], None, kd, cf, sums, 3)
    half = iota((1, 128), 1) < NP
    tot = [lane_totals(sums, k, 0, NP) for k in range(4)]
    ptot[me, 0:1, :] = jnp.where(half, tot[0], pltpu.roll(tot[1], NP, 1))
    ptot[me, 1:2, :] = jnp.where(half, tot[2], pltpu.roll(tot[3], NP, 1))
    p_make, p_made = broadcast(ptot, pt_s, pt_r)
    send_all(p_make)

    wait_all(copies)
    place_rows(v0, NP, NA, arow_r.at[0])
    k_pass(v0, v1, NP, 1, acol_r.at[0, 0], acol_r.at[0, 1], acol_s.at[1], kd, cf, sums, 1, own=0)
    rows_of(v1, NP, NA, arow_s.at[1])
    wait_all(exchange(arow_s, arow_r, acol_s, acol_r, ax_s, ax_r, 1))
    place_rows(v1, NP, NA, arow_r.at[1])
    k_pass(v1, v2, NP, 1, acol_r.at[1, 0], acol_r.at[1, 1], acol_s.at[2], kd, cf, sums, 2)
    rows_of(v2, NP, NA, arow_s.at[2])
    copies = exchange(arow_s, arow_r, acol_s, acol_r, ax_s, ax_r, 2)
    image_copy = pltpu.make_async_copy(
        v2.at[pl.ds(NP, NA), pl.ds(8, ROWS), :], image_out.at[pl.ds(NP, NA)], out_sem.at[2]
    )
    image_copy.start()
    wait_all(copies)
    place_rows(v2, NP, NA, arow_r.at[2])
    k_pass(v2, None, NP, 1, acol_r.at[2, 0], acol_r.at[2, 1], None, kd, cf, sums, 3)
    row = jnp.zeros((1, 128), f32)
    for k in range(4):
        row = row + pltpu.roll(lane_totals(sums, k, NP, NA), NA * k, 1)
    atot[me, 0:1, :] = row
    a_make, a_made = broadcast(atot, at_s, at_r)
    send_all(a_make)
    wait_for(p_made)
    wait_for(a_made)
    pt = jnp.sum(ptot[...], axis=0)
    at = jnp.sum(atot[...], axis=0)

    is_probe = iota((1, 128), 1) < NP
    ps = [pt[0:1], pltpu.roll(pt[0:1], NP, 1), pt[1:2], pltpu.roll(pt[1:2], NP, 1)]
    s0, s1, s2, s3 = [
        jnp.where(is_probe, ps[k], pltpu.roll(at, (NP - NA * k) % 128, 1)) for k in range(4)
    ]
    alpha = jnp.where(s1 > 0.0, s0 / s1, 0.0)
    next_rr = jnp.maximum(alpha * alpha * s2 - s0, 0.0)
    beta = jnp.where(s0 > 0.0, next_rr / s0, 0.0)
    grow = 1.0 + beta
    denom = grow * grow * s1 - 2.0 * grow * alpha * s2 + alpha * alpha * s3
    step = jnp.where(denom > 0.0, next_rr / denom, 0.0)
    step = jnp.minimum(jnp.maximum(step, STEP_MIN), STEP_MAX)
    scale_b, scale_q = alpha + step * grow, -alpha * step
    spot = iota((NF, 128), 1) == iota((NF, 128), 0)
    for k, scale in enumerate((scale_b, scale_q)):
        column = jnp.sum(jnp.where(spot, scale, 0.0), axis=1, keepdims=True)
        scale_out[k] = jnp.broadcast_to(column, (NF, 128))
    probe_out.wait()
    adj_copy.wait()
    image_copy.wait()


def final_kernel(probes, adj, image, scale, out):
    s = pl.program_id(0)

    def combine(field_of):
        for l in range(LEVELS):
            b = field_of(l)
            sb = scale[0, pl.ds(s * LEVELS + l, 1), :]
            sq = scale[1, pl.ds(s * LEVELS + l, 1), :]
            sb, sq = jnp.concatenate([sb, sb], 1), jnp.concatenate([sq, sq], 1)
            out[l] = sb * b + sq * image[l]

    @pl.when(s < 8)
    def _():
        combine(lambda l: probes[l].astype(f32))

    @pl.when(s == 8)
    def _():
        combine(lambda l: adj[l])


def local(probes, kappa, cond_lat, cond_lon, inno, weight, dest, cell):
    vmem = pl.BlockSpec(memory_space=pltpu.VMEM)
    hbm = pl.BlockSpec(memory_space=pl.ANY)
    reg, dma = pltpu.SemaphoreType.REGULAR, pltpu.SemaphoreType.DMA
    probes = probes.reshape(NP, ROWS, COLS)
    buf = lambda *shape: pltpu.VMEM(shape, f32)
    image, adj, scale = pl.pallas_call(
        main_kernel,
        out_shape=[
            jax.ShapeDtypeStruct((NF, ROWS, COLS), f32),
            jax.ShapeDtypeStruct((NA, ROWS, COLS), f32),
            jax.ShapeDtypeStruct((2, NF, 128), f32),
        ],
        in_specs=[vmem] * 8,
        out_specs=[hbm, hbm, vmem],
        scratch_shapes=[
            buf(NF, PAD, COLS), buf(NF, PAD, COLS), buf(NF, PAD, COLS),
            buf(LEVELS * ROWS, COLS), buf(576, 256), buf(1, HELD), buf(DEV, 128),
            buf(DEV, 9, 128), buf(DEV, 9, 128), buf(LEVELS, ROWS, COLS), buf(4, ROWS, COLS), buf(4, NF, 8, 128),
            buf(3, 2, NF, COLS), buf(3, 2, NF, COLS), buf(3, 2, ROWS, 128), buf(3, 2, ROWS, 128),
            buf(3, 2, NA, COLS), buf(3, 2, NA, COLS), buf(3, 2, ROWS, 128), buf(3, 2, ROWS, 128),
            buf(DEV, 2, 128), buf(DEV, 1, 128),
            reg, dma((DEV,)), dma((DEV,)), dma((3, 4)), dma((3, 4)), dma((3, 4)), dma((3, 4)),
            dma((DEV,)), dma((DEV,)), dma((DEV,)), dma((DEV,)), dma((3,)),
        ],
        compiler_params=pltpu.CompilerParams(
            collective_id=0, has_side_effects=True, vmem_limit_bytes=48 * 2**20
        ),
        name="main",
    )(
        probes, kappa, cond_lat, cond_lon, inno, weight.reshape(64, 128), dest.reshape(1, HELD), cell.reshape(64, 128)
    )
    out = pl.pallas_call(
        final_kernel,
        grid=(9,),
        out_shape=jax.ShapeDtypeStruct((NF, ROWS, COLS), f32),
        in_specs=[
            pl.BlockSpec((LEVELS, ROWS, COLS), lambda s: (jnp.minimum(s, 7), 0, 0)),
            pl.BlockSpec((NA, ROWS, COLS), lambda s: (0, 0, 0)),
            pl.BlockSpec((LEVELS, ROWS, COLS), lambda s: (s, 0, 0)),
            pl.BlockSpec((2, NF, 128), lambda s: (0, 0, 0)),
        ],
        out_specs=pl.BlockSpec((LEVELS, ROWS, COLS), lambda s: (s, 0, 0)),
        name="final",
    )(probes, adj, image, scale)
    return out.reshape(9, LEVELS, ROWS, COLS)


def solution(mesh):
    placed = (
        P(None, None, "lat", "lon"),
        P(None, "lat", "lon"),
        P("lat", "lon"),
        P("lat", "lon"),
        P(None, ("lat", "lon")),
        P(("lat", "lon")),
        P(("lat", "lon"), None),
        P(("lat", "lon")),
    )
    return jax.shard_map(
        local, mesh=mesh, in_specs=placed, out_specs=P(None, None, "lat", "lon"), check_vma=False
    )
```

```python
import functools

import jax
import jax.numpy as jnp
from jax import lax
from jax.experimental import pallas as pl
from jax.experimental.pallas import tpu as pltpu
from jax.sharding import PartitionSpec as P

f32, bf16, i32 = jnp.float32, jnp.bfloat16, jnp.int32
MESH = pl.DeviceIdType.MESH
LAT, LON, DEV = 8, 16, 128
LEVELS, ROWS, COLS = 8, 64, 256
NP, NA, NF = 64, 8, 72
PAD = ROWS + 16
HELD, SLOTS = 8192, 128
NT = (((1,), (1,)), ((), ()))
STEP_MIN, STEP_MAX = 1.0 / 25.0, 1.0 / 0.04


def iota(shape, dim):
    return lax.broadcasted_iota(i32, shape, dim)


def split2(v):
    hi = v.astype(bf16)
    return hi, (v - hi.astype(f32)).astype(bf16)


def one_hot(mask):
    return jnp.where(mask, 1.0, 0.0).astype(bf16)


def flat_rows(block, count):
    return jnp.concatenate([block[i : i + 1] for i in range(count)], 1)


def rank_phase(dest, pos, carry, span=256):
    upper = one_hot(iota((span, span), 0) < iota((span, span), 1))
    carry[...] = jnp.zeros((DEV, 128), f32)

    def body(c, _):
        s0 = pl.multiple_of(c * span, span)
        mask = iota((DEV, span), 0) == dest[:, pl.ds(s0, span)]
        hot = jnp.where(mask, 1.0, 0.0)
        within = jnp.dot(hot.astype(bf16), upper, preferred_element_type=f32)
        before = jnp.concatenate([carry[...]] * (span // 128), 1)
        pos[:, pl.ds(s0, span)] = jnp.sum(jnp.where(mask, within + before, 0.0), axis=0, keepdims=True)
        carry[...] += jnp.sum(hot, axis=1, keepdims=True)
        return 0

    lax.fori_loop(0, HELD // span, body, 0, unroll=4)


def pack_phase(inno, weight, dest, cell, pos, acc, send, span=1024):
    acc[...] = jnp.zeros((576, 256), f32)
    part = span // 128

    def body(c, _):
        s0 = pl.multiple_of(c * span, span)
        r0 = pl.multiple_of(c * part, part)
        d = dest[:, pl.ds(s0, span)]
        d_hi = jnp.where(d >= 64, 1, 0)
        d_lo = d - d_hi * 64
        slot = pos[:, pl.ds(s0, span)].astype(i32) + d_hi * SLOTS
        hi, lo = split2(inno[:, pl.ds(s0, span)] * flat_rows(weight[pl.ds(r0, part), :], part))
        cells = flat_rows(cell[pl.ds(r0, part), :], part)
        c_row = cells // COLS
        cell_hi = (c_row * COLS).astype(f32).astype(bf16)
        cell_lo = (cells - c_row * COLS).astype(f32).astype(bf16)
        slot_hot = one_hot(iota((256, span), 0) == slot)
        hi2, lo2 = jnp.concatenate([hi, hi], 0), jnp.concatenate([lo, lo], 0)
        pair = iota((16, span), 0) // 8
        left_hi, left_lo = [], []
        for t in range(32):
            mine = one_hot((pair + 2 * t) == d_lo)
            left_hi.append(mine * hi2)
            left_lo.append(mine * lo2)
        mine = one_hot(iota((64, span), 0) == d_lo)
        left_hi.append(mine * cell_hi)
        left_lo.append(mine * cell_lo)
        acc[...] += lax.dot_general(
            jnp.concatenate(left_hi, 0), slot_hot, NT, preferred_element_type=f32
        ) + lax.dot_general(jnp.concatenate(left_lo, 0), slot_hot, NT, preferred_element_type=f32)
        return 0

    lax.fori_loop(0, HELD // span, body, 0)
    for d in range(DEV):
        lo_d, hi_d = d % 64, d // 64
        at = slice(hi_d * SLOTS, (hi_d + 1) * SLOTS)
        send[d, 0:8, :] = acc[lo_d * 8 : lo_d * 8 + 8, at]
        send[d, 8:9, :] = acc[512 + lo_d : 513 + lo_d, at]


def scatter_phase(got, adj, arrived, group=8):
    adj[...] = jnp.zeros((LEVELS * ROWS, COLS), f32)
    span = group * SLOTS

    def body(g, _):
        sources = arrived(g)
        cells = jnp.concatenate([got[d, 8:9, :] for d in sources], 1).astype(i32)
        vals = jnp.concatenate([got[d, 0:8, :] for d in sources], 1)
        row = cells // COLS
        col_hot = one_hot(iota((COLS, span), 0) == cells - row * COLS)
        row_hot = one_hot(iota((ROWS, span), 0) == (row % 8) * 8 + row // 8)
        hi, lo = split2(vals)
        left_hi = jnp.concatenate([row_hot * hi[l : l + 1] for l in range(LEVELS)], 0)
        left_lo = jnp.concatenate([row_hot * lo[l : l + 1] for l in range(LEVELS)], 0)
        adj[...] += lax.dot_general(left_hi, col_hot, NT, preferred_element_type=f32) + lax.dot_general(
            left_lo, col_hot, NT, preferred_element_type=f32
        )
        return 0

    lax.fori_loop(0, DEV // group, body, 0)


def put_swapped(ref, values):
    for h in range(2):
        for a in range(8):
            ref[h, pl.ds(a, 8, stride=8), :] = values[a * 8 : a * 8 + 8, h * 128 : h * 128 + 128]


def strip_sum(sq):
    return sq[:, :128] + sq[:, 128:]


def k_pass(src, dst, first, span, halo, kd, cf, sums, which, own=None):
    def strip(i, _):
        r0 = pl.multiple_of(i * 8, 8)
        mid, below, above = (pl.multiple_of(r0 + k, 8) for k in (8, 16, 0))
        lane = iota((8, 128), 1)
        at_0, at_127 = lane == 0, lane == 127
        wide = lambda ref, k, at: jnp.concatenate([ref[k, 0, at, :], ref[k, 1, at, :]], 1)
        here = pl.ds(r0, 8)
        north, south, west, east = [wide(cf, k, here) for k in range(4)]
        for n in span:
            f = first + n
            c = wide(src, f, pl.ds(mid, 8))
            cl, cr, beyond = c[:, :128], c[:, 128:], halo[n, here, :]
            left = jnp.concatenate(
                [pltpu.roll(jnp.where(at_127, beyond, cl), 1, 1), pltpu.roll(jnp.where(at_127, cl, cr), 1, 1)], 1
            )
            right = jnp.concatenate(
                [pltpu.roll(jnp.where(at_0, cr, cl), 127, 1), pltpu.roll(jnp.where(at_0, beyond, cr), 127, 1)], 1
            )
            up, down = wide(src, f, pl.ds(above, 8)), wide(src, f, pl.ds(below, 8))
            out = wide(kd, n % 8, here) * c - north * up - south * down - west * left - east * right
            sums[which, f] += strip_sum(out * out)
            if own is not None:
                sums[own, f] += strip_sum(c * c)
            if dst is not None:
                dst[f, 0, pl.ds(mid, 8), :] = out[:, :128]
                dst[f, 1, pl.ds(mid, 8), :] = out[:, 128:]
        return 0

    lax.fori_loop(0, ROWS // 8, strip, 0)


def cols_of(field, first, count, cols_out):
    def strip(i, _):
        r0 = pl.multiple_of(i * 8, 8)
        mid = pl.multiple_of(r0 + 8, 8)
        lane = iota((8, 128), 1)
        edge_l = edge_r = jnp.zeros((8, 128), f32)
        for j in range(count):
            edge_l = jnp.where(lane == j, pltpu.roll(field[first + j, 0, pl.ds(mid, 8), :], j, 1), edge_l)
            edge_r = jnp.where(lane == j, pltpu.roll(field[first + j, 1, pl.ds(mid, 8), :], j + 1, 1), edge_r)
        cols_out[0, pl.ds(r0, 8), :] = edge_r
        cols_out[1, pl.ds(r0, 8), :] = edge_l
        return 0

    lax.fori_loop(0, ROWS // 8, strip, 0)


def place_cols(halo, count, cols_in):
    def strip(i, _):
        here = pl.ds(pl.multiple_of(i * 8, 8), 8)
        lane = iota((8, 128), 1)
        before, after = cols_in[0, here, :], cols_in[1, here, :]
        for j in range(count):
            halo[j, here, :] = jnp.where(
                lane == 127, pltpu.roll(before, 127 - j, 1), pltpu.roll(after, (128 - j) % 128, 1)
            )
        return 0

    lax.fori_loop(0, ROWS // 8, strip, 0)


def rows_of(field, first, count, rows_out):
    for j in range(count):
        for h in range(2):
            at = slice(h * 128, h * 128 + 128)
            rows_out[0, j : j + 1, at] = field[first + j, h, ROWS + 7 : ROWS + 8, :]
            rows_out[1, j : j + 1, at] = field[first + j, h, 8:9, :]


def place_rows(field, first, count, rows_in):
    row = iota((8, 128), 0)
    for j in range(count):
        f = first + j
        for h in range(2):
            at = slice(h * 128, h * 128 + 128)
            last, top = field[f, h, ROWS : ROWS + 8, :], field[f, h, 8:16, :]
            field[f, h, 0:8, :] = jnp.where(row == 0, rows_in[0, j : j + 1, at], pltpu.roll(last, 1, 0))
            field[f, h, ROWS + 8 : ROWS + 16, :] = jnp.where(
                row == 7, rows_in[1, j : j + 1, at], pltpu.roll(top, 7, 0)
            )


def lane_totals(sums, which, first, count):
    part = jnp.sum(sums[which, first : first + count], axis=1)
    total = jnp.sum(part, axis=1, keepdims=True)
    return jnp.sum(jnp.where(iota((count, 128), 1) == iota((count, 128), 0), total, 0.0), axis=0, keepdims=True)


def main_kernel(
    probes_in, kappa_in, cond_lat_in, cond_lon_in, inno_in, weight_in, dest_in, cell_in,
    v0, v2, scale_out,
    v1, adj, acc, pos, carry, send, got, kd, cf, sums,
    prow_s, prow_r, pcol_s, pcol_r, arow_s, arow_r, acol_s, acol_r, tot, phalo, ahalo,
    ready, a2a_s, a2a_r, px_s, px_r, ax_s, ax_r, tot_s, tot_r,
    probes, kappa, cond_lat, cond_lon, inno, weight, dest, cell, in_sem,
):
    la, lo = lax.axis_index("lat"), lax.axis_index("lon")
    me = la * LON + lo
    ins = [
        pltpu.make_async_copy(src, dst, in_sem.at[k])
        for k, (src, dst) in enumerate(
            [
                (probes_in, probes), (cond_lat_in, cond_lat), (cond_lon_in, cond_lon), (dest_in, dest),
                (weight_in, weight), (cell_in, cell), (inno_in, inno), (kappa_in, kappa),
            ]
        )
    ]
    for copy in ins:
        copy.start()
    lat_peers = [(lax.rem(la + i, LAT), lo) for i in range(1, LAT)]
    lon_peers = [(la, lax.rem(lo + i, LON)) for i in range(1, LON)]
    barrier = pltpu.get_barrier_semaphore()
    for peer in lat_peers + lon_peers:
        pl.semaphore_signal(barrier, inc=1, device_id=peer, device_id_type=MESH)

    beside = [lat_peers[0], lat_peers[-1], lon_peers[0], lon_peers[-1]]

    def exchange(rows_s, rows_r, cols_s, cols_r, s_sem, r_sem, k):
        parts = [(rows_s, rows_r, 0), (rows_s, rows_r, 1), (cols_s, cols_r, 0), (cols_s, cols_r, 1)]
        copies = []
        for n, (src, dst, side) in enumerate(parts):
            copies.append(
                pltpu.make_async_remote_copy(
                    src_ref=src.at[k, side], dst_ref=dst.at[k, side], send_sem=s_sem.at[k, n],
                    recv_sem=r_sem.at[k, n], device_id=beside[n], device_id_type=MESH,
                )
            )
            copies[-1].start()
        return copies

    def wait_all(copies):
        for copy in copies:
            copy.wait()

    x, y, z, core = lo // 4, la // 2, lax.rem(lo, 4), lax.rem(la, 2)

    def step_of(a):
        return a + a // 2 - 2 * (a // 3)

    def group_of(g):
        gy, gx = lax.rem(y + step_of(g // 4), 4), lax.rem(x + step_of(lax.rem(g, 4)), 4)
        return [(gy * 2 + lax.rem(core + c, 2)) * LON + gx * 4 + lax.rem(z + dz, 4) for c in range(2) for dz in range(4)]

    def device(d):
        return (d // LON, lax.rem(d, LON))

    def to_all(make):
        for d in group_of(0)[1:]:
            make(d).start()

        def rest(g, _):
            for d in group_of(g):
                make(d).start()
            return 0

        lax.fori_loop(1, DEV // 8, rest, 0)

    def station_copy(src, dst):
        return pltpu.make_async_remote_copy(
            src_ref=send.at[src], dst_ref=got.at[dst], send_sem=a2a_s, recv_sem=a2a_r.at[dst],
            device_id=device(src), device_id_type=MESH,
        )

    def total_copy(d):
        return pltpu.make_async_remote_copy(
            src_ref=tot.at[me], dst_ref=tot.at[me], send_sem=tot_s, recv_sem=tot_r,
            device_id=device(d), device_id_type=MESH,
        )

    sums[...] = jnp.zeros(sums.shape, f32)
    for copy in ins[:3]:
        copy.wait()

    def widen(s, _):
        for l in range(LEVELS):
            f = s * LEVELS + l
            for a in range(4):
                wide = probes[f, a * 16 : a * 16 + 16, :].astype(f32)
                for h in range(2):
                    at = slice(h * 128, h * 128 + 128)
                    v0[f, h, pl.ds(8 + 2 * a, 8, stride=8), :] = wide[:8, at]
                    v0[f, h, pl.ds(9 + 2 * a, 8, stride=8), :] = wide[8:, at]
        return 0

    lax.fori_loop(0, 8, widen, 0)
    cols_of(v0, 0, NP, pcol_s.at[0])
    rows_of(v0, 0, NP, prow_s.at[0])
    lane = iota((ROWS, 128), 1)
    lat_row = iota((ROWS, COLS), 0)
    prow_s[0, 0, NP : NP + 1, :] = cond_lat[ROWS - 1 : ROWS, :]
    put_swapped(cf.at[3], cond_lon[...])
    pcol_s[0, 0] = jnp.where(lane == NP, pltpu.roll(cf[3, 1], NP + 1, 1), pcol_s[0, 0])

    for copy in ins[3:]:
        copy.wait()
    rank_phase(dest, pos, carry)
    pack_phase(inno, weight, dest, cell, pos, acc, send)
    pl.semaphore_wait(barrier, LAT + LON - 2)
    for peer in lon_peers:
        pl.semaphore_signal(ready, inc=1, device_id=peer, device_id_type=MESH)
    copies = exchange(prow_s, prow_r, pcol_s, pcol_r, px_s, px_r, 0)
    got[me] = send[me]
    pl.semaphore_wait(ready, LON - 1)
    to_all(lambda d: station_copy(d, me))

    wait_all(copies)
    put_swapped(
        cf.at[0],
        jnp.where(
            lat_row == 0, jnp.where(la == 0, 0.0, prow_r[0, 0, NP : NP + 1, :]), pltpu.roll(cond_lat[...], 1, 0)
        ),
    )
    put_swapped(cf.at[1], jnp.where((lat_row == ROWS - 1) & (la == LAT - 1), 0.0, cond_lat[...]))
    el, er = cf[3, 0], cf[3, 1]
    cf[2, 0] = jnp.where(lane == 0, pltpu.roll(pcol_r[0, 0], 128 - NP, 1), pltpu.roll(el, 1, 1))
    cf[2, 1] = pltpu.roll(jnp.where(lane == 127, el, er), 1, 1)
    faces = cf[0] + cf[1] + cf[2] + cf[3]
    for l in range(LEVELS):
        put_swapped(kd.at[l], kappa[l])
        kd[l] += faces
    all_p, all_a = range(NP), range(NA)
    place_rows(v0, 0, NP, prow_r.at[0])
    place_cols(phalo, NP, pcol_r.at[0])
    k_pass(v0, v1, 0, all_p, phalo, kd, cf, sums, 1, own=0)
    cols_of(v1, 0, NP, pcol_s.at[1])
    rows_of(v1, 0, NP, prow_s.at[1])
    probe_copies = exchange(prow_s, prow_r, pcol_s, pcol_r, px_s, px_r, 1)

    def arrived(g):
        sources = group_of(g)
        for n, d in enumerate(sources):
            if n:
                station_copy(d, d).wait_recv()
            else:

                @pl.when(g > 0)
                def _():
                    station_copy(d, d).wait_recv()

        return sources

    scatter_phase(got, adj, arrived)
    for l in range(LEVELS):
        for h in range(2):
            v0[NP + l, h, 8 : 8 + ROWS, :] = adj[l * ROWS : (l + 1) * ROWS, h * 128 : h * 128 + 128]
    cols_of(v0, NP, NA, acol_s.at[0])
    rows_of(v0, NP, NA, arow_s.at[0])
    copies = exchange(arow_s, arow_r, acol_s, acol_r, ax_s, ax_r, 0)

    wait_all(probe_copies)
    place_rows(v1, 0, NP, prow_r.at[1])
    place_cols(phalo, NP, pcol_r.at[1])
    k_pass(v1, v2, 0, all_p, phalo, kd, cf, sums, 2)
    cols_of(v2, 0, NP, pcol_s.at[2])
    rows_of(v2, 0, NP, prow_s.at[2])
    probe_copies = exchange(prow_s, prow_r, pcol_s, pcol_r, px_s, px_r, 2)
    wait_all(copies)
    place_rows(v0, NP, NA, arow_r.at[0])
    place_cols(ahalo, NA, acol_r.at[0])
    k_pass(v0, v1, NP, all_a, ahalo, kd, cf, sums, 1, own=0)
    cols_of(v1, NP, NA, acol_s.at[1])
    rows_of(v1, NP, NA, arow_s.at[1])
    copies = exchange(arow_s, arow_r, acol_s, acol_r, ax_s, ax_r, 1)
    wait_all(probe_copies)
    place_rows(v2, 0, NP, prow_r.at[2])
    place_cols(phalo, NP, pcol_r.at[2])
    k_pass(v2, None, 0, range(32), phalo, kd, cf, sums, 3)
    wait_all(copies)
    place_rows(v1, NP, NA, arow_r.at[1])
    place_cols(ahalo, NA, acol_r.at[1])
    k_pass(v1, v2, NP, all_a, ahalo, kd, cf, sums, 2)
    cols_of(v2, NP, NA, acol_s.at[2])
    rows_of(v2, NP, NA, arow_s.at[2])
    copies = exchange(arow_s, arow_r, acol_s, acol_r, ax_s, ax_r, 2)
    k_pass(v2, None, 0, range(32, NP), phalo, kd, cf, sums, 3)
    half = iota((1, 128), 1) < NP
    part = [lane_totals(sums, k, 0, NP) for k in range(4)]
    tot[me, 0:1, :] = jnp.where(half, part[0], pltpu.roll(part[1], NP, 1))
    tot[me, 1:2, :] = jnp.where(half, part[2], pltpu.roll(part[3], NP, 1))
    tot[me, 3:4, :] = jnp.zeros((1, 128), f32)
    wait_all(copies)
    place_rows(v2, NP, NA, arow_r.at[2])
    place_cols(ahalo, NA, acol_r.at[2])
    k_pass(v2, None, NP, all_a, ahalo, kd, cf, sums, 3)
    row = jnp.zeros((1, 128), f32)
    for k in range(4):
        row = row + pltpu.roll(lane_totals(sums, k, NP, NA), NA * k, 1)
    tot[me, 2:3, :] = row

    to_all(total_copy)
    others = pltpu.make_async_remote_copy(
        src_ref=send.at[pl.ds(0, DEV - 1)], dst_ref=got.at[pl.ds(0, DEV - 1)], send_sem=a2a_s, recv_sem=tot_r,
        device_id=lon_peers[0], device_id_type=MESH,
    )
    others.wait_send()
    others = pltpu.make_async_remote_copy(
        src_ref=tot.at[pl.ds(0, DEV - 1)], dst_ref=tot.at[pl.ds(0, DEV - 1)], send_sem=tot_s, recv_sem=tot_r,
        device_id=lon_peers[0], device_id_type=MESH,
    )
    others.wait()
    total = jnp.sum(tot[...], axis=0)
    pt, at = total[0:2], total[2:3]

    is_probe = iota((1, 128), 1) < NP
    ps = [pt[0:1], pltpu.roll(pt[0:1], NP, 1), pt[1:2], pltpu.roll(pt[1:2], NP, 1)]
    s0, s1, s2, s3 = [
        jnp.where(is_probe, ps[k], pltpu.roll(at, (NP - NA * k) % 128, 1)) for k in range(4)
    ]
    alpha = jnp.where(s1 > 0.0, s0 / s1, 0.0)
    next_rr = jnp.maximum(alpha * alpha * s2 - s0, 0.0)
    beta = jnp.where(s0 > 0.0, next_rr / s0, 0.0)
    grow = 1.0 + beta
    denom = grow * grow * s1 - 2.0 * grow * alpha * s2 + alpha * alpha * s3
    step = jnp.where(denom > 0.0, next_rr / denom, 0.0)
    step = jnp.minimum(jnp.maximum(step, STEP_MIN), STEP_MAX)
    scale_b, scale_q = alpha + step * grow, -alpha * step
    spot = iota((NF, 128), 1) == iota((NF, 128), 0)
    for k, scale in enumerate((scale_b, scale_q)):
        column = jnp.sum(jnp.where(spot, scale, 0.0), axis=1, keepdims=True)
        scale_out[k] = jnp.broadcast_to(column, (NF, 128))


def final_kernel(v0, v2, scale, out, block, sem):
    def copy(s, h):
        return pltpu.make_async_copy(block.at[s, :, h], out.at[s, :, :, pl.ds(h * 128, 128)], sem.at[s, h])

    def system(s, _):
        for h in range(2):
            for l in range(LEVELS):
                f = s * LEVELS + l
                sb, sq = scale[0, pl.ds(f, 1), :], scale[1, pl.ds(f, 1), :]
                for t in range(8):
                    at = pl.ds(8 + 8 * t, 8)
                    block[s, l, h, pl.ds(t, 8, stride=8), :] = sb * v0[f, h, at, :] + sq * v2[f, h, at, :]
            copy(s, h).start()
        return 0

    def wait(s, _):
        for h in range(2):
            copy(s, h).wait()
        return 0

    lax.fori_loop(0, 9, system, 0)
    lax.fori_loop(0, 9, wait, 0)


def local(probes, kappa, cond_lat, cond_lon, inno, weight, dest, cell):
    vmem = pl.BlockSpec(memory_space=pltpu.VMEM)
    hbm = pl.BlockSpec(memory_space=pltpu.HBM)
    reg, dma = pltpu.SemaphoreType.REGULAR, pltpu.SemaphoreType.DMA
    probes = probes.reshape(NP, ROWS, COLS)
    weight, cell, dest = weight.reshape(64, 128), cell.reshape(64, 128), dest.reshape(1, HELD)
    args = (probes, kappa, cond_lat, cond_lon, inno, weight, dest, cell)
    buf = lambda *shape: pltpu.VMEM(shape, f32)
    v0, v2, scale = pl.pallas_call(
        main_kernel,
        out_shape=[
            pltpu.VMEM((NF, 2, PAD, 128), f32),
            pltpu.VMEM((NF, 2, PAD, 128), f32),
            pltpu.VMEM((2, NF, 128), f32),
        ],
        in_specs=[hbm] * 8,
        out_specs=[vmem] * 3,
        scratch_shapes=[
            buf(NF, 2, PAD, 128),
            buf(LEVELS * ROWS, COLS), buf(576, 256), buf(1, HELD), buf(DEV, 128),
            buf(DEV, 9, 128), buf(DEV, 9, 128), buf(LEVELS, 2, ROWS, 128), buf(4, 2, ROWS, 128), buf(4, NF, 8, 128),
            buf(3, 2, NF, COLS), buf(3, 2, NF, COLS), buf(3, 2, ROWS, 128), buf(3, 2, ROWS, 128),
            buf(3, 2, NA, COLS), buf(3, 2, NA, COLS), buf(3, 2, ROWS, 128), buf(3, 2, ROWS, 128),
            buf(DEV, 4, 128), buf(NP, ROWS, 128), buf(NA, ROWS, 128),
            reg, dma, dma((DEV,)), dma((3, 4)), dma((3, 4)), dma((3, 4)), dma((3, 4)), dma, dma,
            *[pltpu.VMEM(a.shape, a.dtype) for a in args],
            dma((8,)),
        ],
        compiler_params=pltpu.CompilerParams(
            collective_id=0, has_side_effects=True, vmem_limit_bytes=36 * 2**20
        ),
        name="main",
    )(*[pltpu.with_memory_space_constraint(a, pltpu.HBM) for a in args])
    out = pl.pallas_call(
        final_kernel,
        out_shape=jax.ShapeDtypeStruct((9, LEVELS, ROWS, COLS), f32),
        in_specs=[vmem] * 3,
        out_specs=hbm,
        scratch_shapes=[buf(9, LEVELS, 2, ROWS, 128), dma((9, 2))],
        compiler_params=pltpu.CompilerParams(vmem_limit_bytes=12 * 2**20),
        name="final",
    )(v0, v2, scale)
    return out


def solution(mesh):
    placed = (
        P(None, None, "lat", "lon"),
        P(None, "lat", "lon"),
        P("lat", "lon"),
        P("lat", "lon"),
        P(None, ("lat", "lon")),
        P(("lat", "lon")),
        P(("lat", "lon"), None),
        P(("lat", "lon")),
    )
    return jax.shard_map(
        local, mesh=mesh, in_specs=placed, out_specs=P(None, None, "lat", "lon"), check_vma=False
    )
```

```python
import functools

import jax
import jax.numpy as jnp
from jax import lax
from jax.experimental import pallas as pl
from jax.experimental.pallas import tpu as pltpu
from jax.sharding import PartitionSpec as P

f32, bf16, i32 = jnp.float32, jnp.bfloat16, jnp.int32
MESH = pl.DeviceIdType.MESH
LAT, LON, DEV = 8, 16, 128
LEVELS, ROWS, COLS = 8, 64, 256
NP, NA, NF = 64, 8, 72
PAD = ROWS + 16
HELD, SLOTS = 8192, 128
NT = (((1,), (1,)), ((), ()))
EARLY = 8
STEP_MIN, STEP_MAX = 1.0 / 25.0, 1.0 / 0.04


def iota(shape, dim):
    return lax.broadcasted_iota(i32, shape, dim)


def split2(v):
    hi = v.astype(bf16)
    return hi, (v - hi.astype(f32)).astype(bf16)


def one_hot(mask):
    return jnp.where(mask, 1.0, 0.0).astype(bf16)


def flat_rows(block, count):
    return jnp.concatenate([block[i : i + 1] for i in range(count)], 1)


def rank_phase(dest, pos, carry, span=256):
    upper = one_hot(iota((span, span), 0) < iota((span, span), 1))
    carry[...] = jnp.zeros((DEV, 128), f32)

    def body(c, _):
        s0 = pl.multiple_of(c * span, span)
        mask = iota((DEV, span), 0) == dest[:, pl.ds(s0, span)]
        hot = jnp.where(mask, 1.0, 0.0)
        within = jnp.dot(hot.astype(bf16), upper, preferred_element_type=f32)
        before = jnp.concatenate([carry[...]] * (span // 128), 1)
        pos[:, pl.ds(s0, span)] = jnp.sum(jnp.where(mask, within + before, 0.0), axis=0, keepdims=True)
        carry[...] += jnp.sum(hot, axis=1, keepdims=True)
        return 0

    lax.fori_loop(0, HELD // span, body, 0, unroll=4)


def pack_phase(inno, weight, dest, cell, pos, acc, send, span=1024):
    acc[...] = jnp.zeros((576, 256), f32)
    part = span // 128

    def body(c, _):
        s0 = pl.multiple_of(c * span, span)
        r0 = pl.multiple_of(c * part, part)
        d = dest[:, pl.ds(s0, span)]
        d_hi = jnp.where(d >= 64, 1, 0)
        d_lo = d - d_hi * 64
        slot = pos[:, pl.ds(s0, span)].astype(i32) + d_hi * SLOTS
        hi, lo = split2(inno[:, pl.ds(s0, span)] * flat_rows(weight[pl.ds(r0, part), :], part))
        cells = flat_rows(cell[pl.ds(r0, part), :], part)
        c_row = cells // COLS
        cell_hi = (c_row * COLS).astype(f32).astype(bf16)
        cell_lo = (cells - c_row * COLS).astype(f32).astype(bf16)
        slot_hot = one_hot(iota((256, span), 0) == slot)
        hi2, lo2 = jnp.concatenate([hi, hi], 0), jnp.concatenate([lo, lo], 0)
        pair = iota((16, span), 0) // 8
        left_hi, left_lo = [], []
        for t in range(32):
            mine = one_hot((pair + 2 * t) == d_lo)
            left_hi.append(mine * hi2)
            left_lo.append(mine * lo2)
        mine = one_hot(iota((64, span), 0) == d_lo)
        left_hi.append(mine * cell_hi)
        left_lo.append(mine * cell_lo)
        acc[...] += lax.dot_general(
            jnp.concatenate(left_hi, 0), slot_hot, NT, preferred_element_type=f32
        ) + lax.dot_general(jnp.concatenate(left_lo, 0), slot_hot, NT, preferred_element_type=f32)
        return 0

    lax.fori_loop(0, HELD // span, body, 0)
    for d in range(DEV):
        lo_d, hi_d = d % 64, d // 64
        at = slice(hi_d * SLOTS, (hi_d + 1) * SLOTS)
        send[d, 0:8, :] = acc[lo_d * 8 : lo_d * 8 + 8, at]
        send[d, 8:9, :] = acc[512 + lo_d : 513 + lo_d, at]


def scatter_phase(got, adj, arrived, first, last, group=8):
    span = group * SLOTS

    def body(g, _):
        sources = arrived(g)
        cells = jnp.concatenate([got[d, 8:9, :] for d in sources], 1).astype(i32)
        vals = jnp.concatenate([got[d, 0:8, :] for d in sources], 1)
        row = cells // COLS
        col_hot = one_hot(iota((COLS, span), 0) == cells - row * COLS)
        row_hot = one_hot(iota((ROWS, span), 0) == (row % 8) * 8 + row // 8)
        hi, lo = split2(vals)
        left_hi = jnp.concatenate([row_hot * hi[l : l + 1] for l in range(LEVELS)], 0)
        left_lo = jnp.concatenate([row_hot * lo[l : l + 1] for l in range(LEVELS)], 0)
        adj[...] += lax.dot_general(left_hi, col_hot, NT, preferred_element_type=f32) + lax.dot_general(
            left_lo, col_hot, NT, preferred_element_type=f32
        )
        return 0

    lax.fori_loop(first, last, body, 0)


def put_swapped(ref, values):
    for h in range(2):
        for a in range(8):
            ref[h, pl.ds(a, 8, stride=8), :] = values[a * 8 : a * 8 + 8, h * 128 : h * 128 + 128]


def strip_sum(sq):
    return sq[:, :128] + sq[:, 128:]


def k_pass(src, dst, first, span, halo, kd, cf, sums, which, own=None):
    def strip(i, _):
        r0 = pl.multiple_of(i * 8, 8)
        mid, below, above = (pl.multiple_of(r0 + k, 8) for k in (8, 16, 0))
        lane = iota((8, 128), 1)
        at_0, at_127 = lane == 0, lane == 127
        wide = lambda ref, k, at: jnp.concatenate([ref[k, 0, at, :], ref[k, 1, at, :]], 1)
        here = pl.ds(r0, 8)
        north, south, west, east = [wide(cf, k, here) for k in range(4)]
        for n in span:
            f = first + n
            c = wide(src, f, pl.ds(mid, 8))
            cl, cr, beyond = c[:, :128], c[:, 128:], halo[n, here, :]
            left = jnp.concatenate(
                [pltpu.roll(jnp.where(at_127, beyond, cl), 1, 1), pltpu.roll(jnp.where(at_127, cl, cr), 1, 1)], 1
            )
            right = jnp.concatenate(
                [pltpu.roll(jnp.where(at_0, cr, cl), 127, 1), pltpu.roll(jnp.where(at_0, beyond, cr), 127, 1)], 1
            )
            up, down = wide(src, f, pl.ds(above, 8)), wide(src, f, pl.ds(below, 8))
            out = wide(kd, n % 8, here) * c - north * up - south * down - west * left - east * right
            sums[which, f] += strip_sum(out * out)
            if own is not None:
                sums[own, f] += strip_sum(c * c)
            if dst is not None:
                dst[f, 0, pl.ds(mid, 8), :] = out[:, :128]
                dst[f, 1, pl.ds(mid, 8), :] = out[:, 128:]
        return 0

    lax.fori_loop(0, ROWS // 8, strip, 0, unroll=len(span) <= NA)


def cols_of(field, first, count, cols_out):
    def strip(i, _):
        r0 = pl.multiple_of(i * 8, 8)
        mid = pl.multiple_of(r0 + 8, 8)
        lane = iota((8, 128), 1)
        edge_l = edge_r = jnp.zeros((8, 128), f32)
        for j in range(count):
            edge_l = jnp.where(lane == j, pltpu.roll(field[first + j, 0, pl.ds(mid, 8), :], j, 1), edge_l)
            edge_r = jnp.where(lane == j, pltpu.roll(field[first + j, 1, pl.ds(mid, 8), :], j + 1, 1), edge_r)
        cols_out[0, pl.ds(r0, 8), :] = edge_r
        cols_out[1, pl.ds(r0, 8), :] = edge_l
        return 0

    lax.fori_loop(0, ROWS // 8, strip, 0, unroll=count <= NA)


def place_cols(halo, count, cols_in):
    def strip(i, _):
        here = pl.ds(pl.multiple_of(i * 8, 8), 8)
        lane = iota((8, 128), 1)
        before, after = cols_in[0, here, :], cols_in[1, here, :]
        for j in range(count):
            halo[j, here, :] = jnp.where(
                lane == 127, pltpu.roll(before, 127 - j, 1), pltpu.roll(after, (128 - j) % 128, 1)
            )
        return 0

    lax.fori_loop(0, ROWS // 8, strip, 0, unroll=count <= NA)


def rows_of(field, first, count, rows_out):
    for j in range(count):
        for h in range(2):
            at = slice(h * 128, h * 128 + 128)
            rows_out[0, j : j + 1, at] = field[first + j, h, ROWS + 7 : ROWS + 8, :]
            rows_out[1, j : j + 1, at] = field[first + j, h, 8:9, :]


def place_rows(field, first, count, rows_in):
    row = iota((8, 128), 0)
    for j in range(count):
        f = first + j
        for h in range(2):
            at = slice(h * 128, h * 128 + 128)
            last, top = field[f, h, ROWS : ROWS + 8, :], field[f, h, 8:16, :]
            field[f, h, 0:8, :] = jnp.where(row == 0, rows_in[0, j : j + 1, at], pltpu.roll(last, 1, 0))
            field[f, h, ROWS + 8 : ROWS + 16, :] = jnp.where(
                row == 7, rows_in[1, j : j + 1, at], pltpu.roll(top, 7, 0)
            )


def lane_totals(sums, which, first, count):
    part = jnp.sum(sums[which, first : first + count], axis=1)
    total = jnp.sum(part, axis=1, keepdims=True)
    return jnp.sum(jnp.where(iota((count, 128), 1) == iota((count, 128), 0), total, 0.0), axis=0, keepdims=True)


def main_kernel(
    probes_in, kappa_in, cond_lat_in, cond_lon_in, inno_in, weight_in, dest_in, cell_in,
    v0, v2, scale_out,
    v1, adj, acc, pos, carry, send, got, kd, cf, sums,
    prow_s, prow_r, pcol_s, pcol_r, arow_s, arow_r, acol_s, acol_r, tot, phalo, ahalo,
    ready, a2a_s, a2a_r, px_s, px_r, ax_s, ax_r, tot_s, tot_r,
    probes, kappa, cond_lat, cond_lon, inno, weight, dest, cell, in_sem,
):
    la, lo = lax.axis_index("lat"), lax.axis_index("lon")
    me = la * LON + lo
    ins = [
        pltpu.make_async_copy(src, dst, in_sem.at[k])
        for k, (src, dst) in enumerate(
            [
                (probes_in, probes), (cond_lat_in, cond_lat), (cond_lon_in, cond_lon), (dest_in, dest),
                (weight_in, weight), (cell_in, cell), (inno_in, inno), (kappa_in, kappa),
            ]
        )
    ]
    for copy in ins:
        copy.start()
    lat_peers = [(lax.rem(la + i, LAT), lo) for i in range(1, LAT)]
    lon_peers = [(la, lax.rem(lo + i, LON)) for i in range(1, LON)]
    barrier = pltpu.get_barrier_semaphore()
    for peer in lat_peers + lon_peers:
        pl.semaphore_signal(barrier, inc=1, device_id=peer, device_id_type=MESH)

    beside = [lat_peers[0], lat_peers[-1], lon_peers[0], lon_peers[-1]]

    def exchange(rows_s, rows_r, cols_s, cols_r, s_sem, r_sem, k):
        parts = [(rows_s, rows_r, 0), (rows_s, rows_r, 1), (cols_s, cols_r, 0), (cols_s, cols_r, 1)]
        copies = []
        for n, (src, dst, side) in enumerate(parts):
            copies.append(
                pltpu.make_async_remote_copy(
                    src_ref=src.at[k, side], dst_ref=dst.at[k, side], send_sem=s_sem.at[k, n],
                    recv_sem=r_sem.at[k, n], device_id=beside[n], device_id_type=MESH,
                )
            )
            copies[-1].start()
        return copies

    def wait_all(copies):
        for copy in copies:
            copy.wait()

    x, y, z, core = lo // 4, la // 2, lax.rem(lo, 4), lax.rem(la, 2)

    def step_of(a):
        return a + a // 2 - 2 * (a // 3)

    def group_of(g):
        gy, gx = lax.rem(y + step_of(g // 4), 4), lax.rem(x + step_of(lax.rem(g, 4)), 4)
        return [(gy * 2 + lax.rem(core + c, 2)) * LON + gx * 4 + lax.rem(z + dz, 4) for c in range(2) for dz in range(4)]

    def device(d):
        return (d // LON, lax.rem(d, LON))

    def to_all(make):
        for d in group_of(0)[1:]:
            make(d).start()

        def rest(g, _):
            for d in group_of(g):
                make(d).start()
            return 0

        lax.fori_loop(1, DEV // 8, rest, 0)

    def station_copy(src, dst):
        return pltpu.make_async_remote_copy(
            src_ref=send.at[src], dst_ref=got.at[dst], send_sem=a2a_s, recv_sem=a2a_r.at[dst],
            device_id=device(src), device_id_type=MESH,
        )

    def total_copy(d):
        return pltpu.make_async_remote_copy(
            src_ref=tot.at[me], dst_ref=tot.at[me], send_sem=tot_s, recv_sem=tot_r,
            device_id=device(d), device_id_type=MESH,
        )

    sums[...] = jnp.zeros(sums.shape, f32)
    for copy in ins[:3]:
        copy.wait()

    def widen(s, _):
        for l in range(LEVELS):
            f = s * LEVELS + l
            for a in range(4):
                wide = probes[f, a * 16 : a * 16 + 16, :].astype(f32)
                for h in range(2):
                    at = slice(h * 128, h * 128 + 128)
                    v0[f, h, pl.ds(8 + 2 * a, 8, stride=8), :] = wide[:8, at]
                    v0[f, h, pl.ds(9 + 2 * a, 8, stride=8), :] = wide[8:, at]
        return 0

    lax.fori_loop(0, 8, widen, 0)
    cols_of(v0, 0, NP, pcol_s.at[0])
    rows_of(v0, 0, NP, prow_s.at[0])
    lane = iota((ROWS, 128), 1)
    lat_row = iota((ROWS, COLS), 0)
    prow_s[0, 0, NP : NP + 1, :] = cond_lat[ROWS - 1 : ROWS, :]
    put_swapped(cf.at[3], cond_lon[...])
    pcol_s[0, 0] = jnp.where(lane == NP, pltpu.roll(cf[3, 1], NP + 1, 1), pcol_s[0, 0])

    for copy in ins[3:]:
        copy.wait()
    rank_phase(dest, pos, carry)
    pl.semaphore_wait(barrier, LAT + LON - 2)
    for peer in lon_peers:
        pl.semaphore_signal(ready, inc=1, device_id=peer, device_id_type=MESH)
    copies = exchange(prow_s, prow_r, pcol_s, pcol_r, px_s, px_r, 0)
    pack_phase(inno, weight, dest, cell, pos, acc, send)
    got[me] = send[me]
    pl.semaphore_wait(ready, LON - 1)
    to_all(lambda d: station_copy(d, me))

    wait_all(copies)
    put_swapped(
        cf.at[0],
        jnp.where(
            lat_row == 0, jnp.where(la == 0, 0.0, prow_r[0, 0, NP : NP + 1, :]), pltpu.roll(cond_lat[...], 1, 0)
        ),
    )
    put_swapped(cf.at[1], jnp.where((lat_row == ROWS - 1) & (la == LAT - 1), 0.0, cond_lat[...]))
    el, er = cf[3, 0], cf[3, 1]
    cf[2, 0] = jnp.where(lane == 0, pltpu.roll(pcol_r[0, 0], 128 - NP, 1), pltpu.roll(el, 1, 1))
    cf[2, 1] = pltpu.roll(jnp.where(lane == 127, el, er), 1, 1)
    faces = cf[0] + cf[1] + cf[2] + cf[3]
    for l in range(LEVELS):
        put_swapped(kd.at[l], kappa[l])
        kd[l] += faces
    all_p, all_a = range(NP), range(NA)
    place_rows(v0, 0, NP, prow_r.at[0])
    place_cols(phalo, NP, pcol_r.at[0])
    k_pass(v0, v1, 0, all_p, phalo, kd, cf, sums, 1, own=0)
    cols_of(v1, 0, NP, pcol_s.at[1])
    rows_of(v1, 0, NP, prow_s.at[1])
    probe_copies = exchange(prow_s, prow_r, pcol_s, pcol_r, px_s, px_r, 1)

    def arrived(g):
        sources = group_of(g)
        for n, d in enumerate(sources):
            if n:
                station_copy(d, d).wait_recv()
            else:

                @pl.when(g > 0)
                def _():
                    station_copy(d, d).wait_recv()

        return sources

    adj[...] = jnp.zeros((LEVELS * ROWS, COLS), f32)
    scatter_phase(got, adj, arrived, 0, EARLY)
    wait_all(probe_copies)
    place_rows(v1, 0, NP, prow_r.at[1])
    place_cols(phalo, NP, pcol_r.at[1])
    k_pass(v1, v2, 0, all_p, phalo, kd, cf, sums, 2)
    cols_of(v2, 0, NP, pcol_s.at[2])
    rows_of(v2, 0, NP, prow_s.at[2])
    probe_copies = exchange(prow_s, prow_r, pcol_s, pcol_r, px_s, px_r, 2)
    scatter_phase(got, adj, arrived, EARLY, DEV // 8)
    for l in range(LEVELS):
        for h in range(2):
            v0[NP + l, h, 8 : 8 + ROWS, :] = adj[l * ROWS : (l + 1) * ROWS, h * 128 : h * 128 + 128]
    cols_of(v0, NP, NA, acol_s.at[0])
    rows_of(v0, NP, NA, arow_s.at[0])
    copies = exchange(arow_s, arow_r, acol_s, acol_r, ax_s, ax_r, 0)

    wait_all(probe_copies)
    place_rows(v2, 0, NP, prow_r.at[2])
    place_cols(phalo, NP, pcol_r.at[2])
    k_pass(v2, None, 0, range(32), phalo, kd, cf, sums, 3)
    wait_all(copies)
    place_rows(v0, NP, NA, arow_r.at[0])
    place_cols(ahalo, NA, acol_r.at[0])
    k_pass(v0, v1, NP, all_a, ahalo, kd, cf, sums, 1, own=0)
    cols_of(v1, NP, NA, acol_s.at[1])
    rows_of(v1, NP, NA, arow_s.at[1])
    copies = exchange(arow_s, arow_r, acol_s, acol_r, ax_s, ax_r, 1)
    k_pass(v2, None, 0, range(32, NP), phalo, kd, cf, sums, 3)
    wait_all(copies)
    place_rows(v1, NP, NA, arow_r.at[1])
    place_cols(ahalo, NA, acol_r.at[1])
    k_pass(v1, v2, NP, all_a, ahalo, kd, cf, sums, 2)
    cols_of(v2, NP, NA, acol_s.at[2])
    rows_of(v2, NP, NA, arow_s.at[2])
    copies = exchange(arow_s, arow_r, acol_s, acol_r, ax_s, ax_r, 2)
    half = iota((1, 128), 1) < NP
    part = [lane_totals(sums, k, 0, NP) for k in range(4)]
    tot[me, 0:1, :] = jnp.where(half, part[0], pltpu.roll(part[1], NP, 1))
    tot[me, 1:2, :] = jnp.where(half, part[2], pltpu.roll(part[3], NP, 1))
    tot[me, 3:4, :] = jnp.zeros((1, 128), f32)
    wait_all(copies)
    place_rows(v2, NP, NA, arow_r.at[2])
    place_cols(ahalo, NA, acol_r.at[2])
    k_pass(v2, None, NP, all_a, ahalo, kd, cf, sums, 3)
    row = jnp.zeros((1, 128), f32)
    for k in range(4):
        row = row + pltpu.roll(lane_totals(sums, k, NP, NA), NA * k, 1)
    tot[me, 2:3, :] = row

    to_all(total_copy)
    others = pltpu.make_async_remote_copy(
        src_ref=send.at[pl.ds(0, DEV - 1)], dst_ref=got.at[pl.ds(0, DEV - 1)], send_sem=a2a_s, recv_sem=tot_r,
        device_id=lon_peers[0], device_id_type=MESH,
    )
    others.wait_send()
    others = pltpu.make_async_remote_copy(
        src_ref=tot.at[pl.ds(0, DEV - 1)], dst_ref=tot.at[pl.ds(0, DEV - 1)], send_sem=tot_s, recv_sem=tot_r,
        device_id=lon_peers[0], device_id_type=MESH,
    )
    others.wait()
    total = jnp.sum(tot[...], axis=0)
    pt, at = total[0:2], total[2:3]

    is_probe = iota((1, 128), 1) < NP
    ps = [pt[0:1], pltpu.roll(pt[0:1], NP, 1), pt[1:2], pltpu.roll(pt[1:2], NP, 1)]
    s0, s1, s2, s3 = [
        jnp.where(is_probe, ps[k], pltpu.roll(at, (NP - NA * k) % 128, 1)) for k in range(4)
    ]
    alpha = jnp.where(s1 > 0.0, s0 / s1, 0.0)
    next_rr = jnp.maximum(alpha * alpha * s2 - s0, 0.0)
    beta = jnp.where(s0 > 0.0, next_rr / s0, 0.0)
    grow = 1.0 + beta
    denom = grow * grow * s1 - 2.0 * grow * alpha * s2 + alpha * alpha * s3
    step = jnp.where(denom > 0.0, next_rr / denom, 0.0)
    step = jnp.minimum(jnp.maximum(step, STEP_MIN), STEP_MAX)
    scale_b, scale_q = alpha + step * grow, -alpha * step
    spot = iota((NF, 128), 1) == iota((NF, 128), 0)
    for k, scale in enumerate((scale_b, scale_q)):
        column = jnp.sum(jnp.where(spot, scale, 0.0), axis=1, keepdims=True)
        scale_out[k] = jnp.broadcast_to(column, (NF, 128))


def final_kernel(v0, v2, scale, out, block, sem):
    def copy(s, h):
        return pltpu.make_async_copy(block.at[s, :, h], out.at[s, :, :, pl.ds(h * 128, 128)], sem.at[s, h])

    def system(s, _):
        for h in range(2):
            for l in range(LEVELS):
                f = s * LEVELS + l
                sb, sq = scale[0, pl.ds(f, 1), :], scale[1, pl.ds(f, 1), :]
                for t in range(8):
                    at = pl.ds(8 + 8 * t, 8)
                    block[s, l, h, pl.ds(t, 8, stride=8), :] = sb * v0[f, h, at, :] + sq * v2[f, h, at, :]
            copy(s, h).start()
        return 0

    def wait(s, _):
        for h in range(2):
            copy(s, h).wait()
        return 0

    lax.fori_loop(0, 9, system, 0)
    lax.fori_loop(0, 9, wait, 0)


def local(probes, kappa, cond_lat, cond_lon, inno, weight, dest, cell):
    vmem = pl.BlockSpec(memory_space=pltpu.VMEM)
    hbm = pl.BlockSpec(memory_space=pltpu.HBM)
    reg, dma = pltpu.SemaphoreType.REGULAR, pltpu.SemaphoreType.DMA
    probes = probes.reshape(NP, ROWS, COLS)
    weight, cell, dest = weight.reshape(64, 128), cell.reshape(64, 128), dest.reshape(1, HELD)
    args = (probes, kappa, cond_lat, cond_lon, inno, weight, dest, cell)
    buf = lambda *shape: pltpu.VMEM(shape, f32)
    v0, v2, scale = pl.pallas_call(
        main_kernel,
        out_shape=[
            pltpu.VMEM((NF, 2, PAD, 128), f32),
            pltpu.VMEM((NF, 2, PAD, 128), f32),
            pltpu.VMEM((2, NF, 128), f32),
        ],
        in_specs=[hbm] * 8,
        out_specs=[vmem] * 3,
        scratch_shapes=[
            buf(NF, 2, PAD, 128),
            buf(LEVELS * ROWS, COLS), buf(576, 256), buf(1, HELD), buf(DEV, 128),
            buf(DEV, 9, 128), buf(DEV, 9, 128), buf(LEVELS, 2, ROWS, 128), buf(4, 2, ROWS, 128), buf(4, NF, 8, 128),
            buf(3, 2, NF, COLS), buf(3, 2, NF, COLS), buf(3, 2, ROWS, 128), buf(3, 2, ROWS, 128),
            buf(3, 2, NA, COLS), buf(3, 2, NA, COLS), buf(3, 2, ROWS, 128), buf(3, 2, ROWS, 128),
            buf(DEV, 4, 128), buf(NP, ROWS, 128), buf(NA, ROWS, 128),
            reg, dma, dma((DEV,)), dma((3, 4)), dma((3, 4)), dma((3, 4)), dma((3, 4)), dma, dma,
            *[pltpu.VMEM(a.shape, a.dtype) for a in args],
            dma((8,)),
        ],
        compiler_params=pltpu.CompilerParams(
            collective_id=0, has_side_effects=True, vmem_limit_bytes=36 * 2**20
        ),
        name="main",
    )(*[pltpu.with_memory_space_constraint(a, pltpu.HBM) for a in args])
    out = pl.pallas_call(
        final_kernel,
        out_shape=jax.ShapeDtypeStruct((9, LEVELS, ROWS, COLS), f32),
        in_specs=[vmem] * 3,
        out_specs=hbm,
        scratch_shapes=[buf(9, LEVELS, 2, ROWS, 128), dma((9, 2))],
        compiler_params=pltpu.CompilerParams(vmem_limit_bytes=12 * 2**20),
        name="final",
    )(v0, v2, scale)
    return out


def solution(mesh):
    placed = (
        P(None, None, "lat", "lon"),
        P(None, "lat", "lon"),
        P("lat", "lon"),
        P("lat", "lon"),
        P(None, ("lat", "lon")),
        P(("lat", "lon")),
        P(("lat", "lon"), None),
        P(("lat", "lon")),
    )
    return jax.shard_map(
        local, mesh=mesh, in_specs=placed, out_specs=P(None, None, "lat", "lon"), check_vma=False
    )
```

```python
import functools

import jax
import jax.numpy as jnp
from jax import lax
from jax.experimental import pallas as pl
from jax.experimental.pallas import tpu as pltpu
from jax.sharding import PartitionSpec as P

f32, bf16, i32 = jnp.float32, jnp.bfloat16, jnp.int32
MESH = pl.DeviceIdType.MESH
LAT, LON, DEV = 8, 16, 128
LEVELS, ROWS, COLS = 8, 64, 256
NP, NA, NF = 64, 8, 72
PAD = ROWS + 16
HELD, SLOTS = 8192, 128
NT = (((1,), (1,)), ((), ()))
EARLY = 8
STEP_MIN, STEP_MAX = 1.0 / 25.0, 1.0 / 0.04


def iota(shape, dim):
    return lax.broadcasted_iota(i32, shape, dim)


def split2(v):
    hi = v.astype(bf16)
    return hi, (v - hi.astype(f32)).astype(bf16)


def one_hot(mask):
    return jnp.where(mask, 1.0, 0.0).astype(bf16)


def flat_rows(block, count):
    return jnp.concatenate([block[i : i + 1] for i in range(count)], 1)


def rank_phase(dest, pos, carry, span=256):
    upper = one_hot(iota((span, span), 0) < iota((span, span), 1))
    carry[...] = jnp.zeros((DEV, 128), f32)

    def body(c, _):
        s0 = pl.multiple_of(c * span, span)
        mask = iota((DEV, span), 0) == dest[:, pl.ds(s0, span)]
        hot = jnp.where(mask, 1.0, 0.0)
        within = jnp.dot(hot.astype(bf16), upper, preferred_element_type=f32)
        before = jnp.concatenate([carry[...]] * (span // 128), 1)
        pos[:, pl.ds(s0, span)] = jnp.sum(jnp.where(mask, within + before, 0.0), axis=0, keepdims=True)
        carry[...] += jnp.sum(hot, axis=1, keepdims=True)
        return 0

    lax.fori_loop(0, HELD // span, body, 0, unroll=4)


def pack_phase(inno, weight, dest, cell, pos, acc, send, span=1024):
    acc[...] = jnp.zeros((576, 256), f32)
    part = span // 128

    def body(c, _):
        s0 = pl.multiple_of(c * span, span)
        r0 = pl.multiple_of(c * part, part)
        d = dest[:, pl.ds(s0, span)]
        d_hi = jnp.where(d >= 64, 1, 0)
        d_lo = d - d_hi * 64
        slot = pos[:, pl.ds(s0, span)].astype(i32) + d_hi * SLOTS
        hi, lo = split2(inno[:, pl.ds(s0, span)] * flat_rows(weight[pl.ds(r0, part), :], part))
        cells = flat_rows(cell[pl.ds(r0, part), :], part)
        c_row = cells // COLS
        cell_hi = (c_row * COLS).astype(f32).astype(bf16)
        cell_lo = (cells - c_row * COLS).astype(f32).astype(bf16)
        slot_hot = one_hot(iota((256, span), 0) == slot)
        hi2, lo2 = jnp.concatenate([hi, hi], 0), jnp.concatenate([lo, lo], 0)
        pair = iota((16, span), 0) // 8
        left_hi, left_lo = [], []
        for t in range(32):
            mine = one_hot((pair + 2 * t) == d_lo)
            left_hi.append(mine * hi2)
            left_lo.append(mine * lo2)
        mine = one_hot(iota((64, span), 0) == d_lo)
        left_hi.append(mine * cell_hi)
        left_lo.append(mine * cell_lo)
        acc[...] += lax.dot_general(
            jnp.concatenate(left_hi, 0), slot_hot, NT, preferred_element_type=f32
        ) + lax.dot_general(jnp.concatenate(left_lo, 0), slot_hot, NT, preferred_element_type=f32)
        return 0

    lax.fori_loop(0, HELD // span, body, 0)
    for d in range(DEV):
        lo_d, hi_d = d % 64, d // 64
        at = slice(hi_d * SLOTS, (hi_d + 1) * SLOTS)
        send[d, 0:8, :] = acc[lo_d * 8 : lo_d * 8 + 8, at]
        send[d, 8:9, :] = acc[512 + lo_d : 513 + lo_d, at]


def scatter_phase(got, adj, arrived, first, last, group=8):
    span = group * SLOTS

    def body(g, _):
        sources = arrived(g)
        cells = jnp.concatenate([got[d, 8:9, :] for d in sources], 1).astype(i32)
        vals = jnp.concatenate([got[d, 0:8, :] for d in sources], 1)
        row = cells // COLS
        col_hot = one_hot(iota((COLS, span), 0) == cells - row * COLS)
        row_hot = one_hot(iota((ROWS, span), 0) == (row % 8) * 8 + row // 8)
        hi, lo = split2(vals)
        left_hi = jnp.concatenate([row_hot * hi[l : l + 1] for l in range(LEVELS)], 0)
        left_lo = jnp.concatenate([row_hot * lo[l : l + 1] for l in range(LEVELS)], 0)
        adj[...] += lax.dot_general(left_hi, col_hot, NT, preferred_element_type=f32) + lax.dot_general(
            left_lo, col_hot, NT, preferred_element_type=f32
        )
        return 0

    lax.fori_loop(first, last, body, 0)


def put_swapped(ref, values):
    for h in range(2):
        for a in range(8):
            ref[h, pl.ds(a, 8, stride=8), :] = values[a * 8 : a * 8 + 8, h * 128 : h * 128 + 128]


def strip_sum(sq):
    return sq[:, :128] + sq[:, 128:]


def k_pass(src, dst, first, span, halo, kd, cf, sums, which, own=None):
    def strip(i, _):
        r0 = pl.multiple_of(i * 8, 8)
        mid, below, above = (pl.multiple_of(r0 + k, 8) for k in (8, 16, 0))
        lane = iota((8, 128), 1)
        at_0, at_127 = lane == 0, lane == 127
        wide = lambda ref, k, at: jnp.concatenate([ref[k, 0, at, :], ref[k, 1, at, :]], 1)
        here = pl.ds(r0, 8)
        north, south, west, east = [wide(cf, k, here) for k in range(4)]
        for n in span:
            f = first + n
            c = wide(src, f, pl.ds(mid, 8))
            cl, cr, beyond = c[:, :128], c[:, 128:], halo[n, here, :]
            left = jnp.concatenate(
                [pltpu.roll(jnp.where(at_127, beyond, cl), 1, 1), pltpu.roll(jnp.where(at_127, cl, cr), 1, 1)], 1
            )
            right = jnp.concatenate(
                [pltpu.roll(jnp.where(at_0, cr, cl), 127, 1), pltpu.roll(jnp.where(at_0, beyond, cr), 127, 1)], 1
            )
            up, down = wide(src, f, pl.ds(above, 8)), wide(src, f, pl.ds(below, 8))
            out = wide(kd, n % 8, here) * c - north * up - south * down - west * left - east * right
            sums[which, f] += strip_sum(out * out)
            if own is not None:
                sums[own, f] += strip_sum(c * c)
            if dst is not None:
                dst[f, 0, pl.ds(mid, 8), :] = out[:, :128]
                dst[f, 1, pl.ds(mid, 8), :] = out[:, 128:]
        return 0

    lax.fori_loop(0, ROWS // 8, strip, 0, unroll=len(span) <= NA)


def cols_of(field, first, count, cols_out):
    def strip(i, _):
        r0 = pl.multiple_of(i * 8, 8)
        mid = pl.multiple_of(r0 + 8, 8)
        lane = iota((8, 128), 1)
        edge_l = edge_r = jnp.zeros((8, 128), f32)
        for j in range(count):
            edge_l = jnp.where(lane == j, pltpu.roll(field[first + j, 0, pl.ds(mid, 8), :], j, 1), edge_l)
            edge_r = jnp.where(lane == j, pltpu.roll(field[first + j, 1, pl.ds(mid, 8), :], j + 1, 1), edge_r)
        cols_out[0, pl.ds(r0, 8), :] = edge_r
        cols_out[1, pl.ds(r0, 8), :] = edge_l
        return 0

    lax.fori_loop(0, ROWS // 8, strip, 0, unroll=count <= NA)


def place_cols(halo, count, cols_in):
    def strip(i, _):
        here = pl.ds(pl.multiple_of(i * 8, 8), 8)
        lane = iota((8, 128), 1)
        before, after = cols_in[0, here, :], cols_in[1, here, :]
        for j in range(count):
            halo[j, here, :] = jnp.where(
                lane == 127, pltpu.roll(before, 127 - j, 1), pltpu.roll(after, (128 - j) % 128, 1)
            )
        return 0

    lax.fori_loop(0, ROWS // 8, strip, 0, unroll=count <= NA)


def rows_of(field, first, count, rows_out):
    for j in range(count):
        for h in range(2):
            at = slice(h * 128, h * 128 + 128)
            rows_out[0, j : j + 1, at] = field[first + j, h, ROWS + 7 : ROWS + 8, :]
            rows_out[1, j : j + 1, at] = field[first + j, h, 8:9, :]


def place_rows(field, first, count, rows_in):
    row = iota((8, 128), 0)
    for j in range(count):
        f = first + j
        for h in range(2):
            at = slice(h * 128, h * 128 + 128)
            last, top = field[f, h, ROWS : ROWS + 8, :], field[f, h, 8:16, :]
            field[f, h, 0:8, :] = jnp.where(row == 0, rows_in[0, j : j + 1, at], pltpu.roll(last, 1, 0))
            field[f, h, ROWS + 8 : ROWS + 16, :] = jnp.where(
                row == 7, rows_in[1, j : j + 1, at], pltpu.roll(top, 7, 0)
            )


def lane_totals(sums, which, first, count):
    part = jnp.sum(sums[which, first : first + count], axis=1)
    total = jnp.sum(part, axis=1, keepdims=True)
    return jnp.sum(jnp.where(iota((count, 128), 1) == iota((count, 128), 0), total, 0.0), axis=0, keepdims=True)


def main_kernel(
    probes_in, kappa_in, cond_lat_in, cond_lon_in, inno_in, weight_in, dest_in, cell_in,
    v0, v2, scale_out,
    v1, adj, acc, pos, carry, send, got, kd, cf, sums,
    prow_s, prow_r, pcol_s, pcol_r, arow_s, arow_r, acol_s, acol_r, tot, phalo, ahalo,
    ready, a2a_s, a2a_r, px_s, px_r, ax_s, ax_r, tot_s, tot_r,
    probes, kappa, cond_lat, cond_lon, inno, weight, dest, cell, in_sem,
):
    la, lo = lax.axis_index("lat"), lax.axis_index("lon")
    me = la * LON + lo
    ins = [
        pltpu.make_async_copy(src, dst, in_sem.at[k])
        for k, (src, dst) in enumerate(
            [
                (probes_in, probes), (cond_lat_in, cond_lat), (cond_lon_in, cond_lon), (dest_in, dest),
                (weight_in, weight), (cell_in, cell), (inno_in, inno), (kappa_in, kappa),
            ]
        )
    ]
    for copy in ins:
        copy.start()
    lat_peers = [(lax.rem(la + i, LAT), lo) for i in range(1, LAT)]
    lon_peers = [(la, lax.rem(lo + i, LON)) for i in range(1, LON)]
    barrier = pltpu.get_barrier_semaphore()
    for peer in lat_peers + lon_peers:
        pl.semaphore_signal(barrier, inc=1, device_id=peer, device_id_type=MESH)

    beside = [lat_peers[0], lat_peers[-1], lon_peers[0], lon_peers[-1]]

    def exchange(rows_s, rows_r, cols_s, cols_r, s_sem, r_sem, k):
        parts = [(rows_s, rows_r, 0), (rows_s, rows_r, 1), (cols_s, cols_r, 0), (cols_s, cols_r, 1)]
        copies = []
        for n, (src, dst, side) in enumerate(parts):
            copies.append(
                pltpu.make_async_remote_copy(
                    src_ref=src.at[k, side], dst_ref=dst.at[k, side], send_sem=s_sem.at[k, n],
                    recv_sem=r_sem.at[k, n], device_id=beside[n], device_id_type=MESH,
                )
            )
            copies[-1].start()
        return copies

    def wait_all(copies):
        for copy in copies:
            copy.wait()

    x, y, z, core = lo // 4, la // 2, lax.rem(lo, 4), lax.rem(la, 2)

    def step_of(a):
        return a + a // 2 - 2 * (a // 3)

    def group_of(g):
        gy, gx = lax.rem(y + step_of(g // 4), 4), lax.rem(x + step_of(lax.rem(g, 4)), 4)
        return [(gy * 2 + lax.rem(core + c, 2)) * LON + gx * 4 + lax.rem(z + dz, 4) for c in range(2) for dz in range(4)]

    def device(d):
        return (d // LON, lax.rem(d, LON))

    def to_all(make, far_first=False):
        def near():
            for d in group_of(0)[1:]:
                make(d).start()

        def rest(g, _):
            for d in group_of(DEV // 8 - g if far_first else g):
                make(d).start()
            return 0

        if not far_first:
            near()
        lax.fori_loop(1, DEV // 8, rest, 0)
        if far_first:
            near()

    def station_copy(src, dst):
        return pltpu.make_async_remote_copy(
            src_ref=send.at[src], dst_ref=got.at[dst], send_sem=a2a_s, recv_sem=a2a_r.at[dst],
            device_id=device(src), device_id_type=MESH,
        )

    def total_copy(d):
        return pltpu.make_async_remote_copy(
            src_ref=tot.at[me], dst_ref=tot.at[me], send_sem=tot_s, recv_sem=tot_r,
            device_id=device(d), device_id_type=MESH,
        )

    sums[...] = jnp.zeros(sums.shape, f32)
    for copy in ins[:3]:
        copy.wait()

    def widen(s, _):
        for l in range(LEVELS):
            f = s * LEVELS + l
            for a in range(4):
                wide = probes[f, a * 16 : a * 16 + 16, :].astype(f32)
                for h in range(2):
                    at = slice(h * 128, h * 128 + 128)
                    v0[f, h, pl.ds(8 + 2 * a, 8, stride=8), :] = wide[:8, at]
                    v0[f, h, pl.ds(9 + 2 * a, 8, stride=8), :] = wide[8:, at]
        return 0

    lax.fori_loop(0, 8, widen, 0)
    cols_of(v0, 0, NP, pcol_s.at[0])
    rows_of(v0, 0, NP, prow_s.at[0])
    lane = iota((ROWS, 128), 1)
    lat_row = iota((ROWS, COLS), 0)
    prow_s[0, 0, NP : NP + 1, :] = cond_lat[ROWS - 1 : ROWS, :]
    put_swapped(cf.at[3], cond_lon[...])
    pcol_s[0, 0] = jnp.where(lane == NP, pltpu.roll(cf[3, 1], NP + 1, 1), pcol_s[0, 0])

    for copy in ins[3:]:
        copy.wait()
    rank_phase(dest, pos, carry)
    pl.semaphore_wait(barrier, LAT + LON - 2)
    for peer in lon_peers:
        pl.semaphore_signal(ready, inc=1, device_id=peer, device_id_type=MESH)
    copies = exchange(prow_s, prow_r, pcol_s, pcol_r, px_s, px_r, 0)
    pack_phase(inno, weight, dest, cell, pos, acc, send)
    got[me] = send[me]
    pl.semaphore_wait(ready, LON - 1)
    to_all(lambda d: station_copy(d, me))

    wait_all(copies)
    put_swapped(
        cf.at[0],
        jnp.where(
            lat_row == 0, jnp.where(la == 0, 0.0, prow_r[0, 0, NP : NP + 1, :]), pltpu.roll(cond_lat[...], 1, 0)
        ),
    )
    put_swapped(cf.at[1], jnp.where((lat_row == ROWS - 1) & (la == LAT - 1), 0.0, cond_lat[...]))
    el, er = cf[3, 0], cf[3, 1]
    cf[2, 0] = jnp.where(lane == 0, pltpu.roll(pcol_r[0, 0], 128 - NP, 1), pltpu.roll(el, 1, 1))
    cf[2, 1] = pltpu.roll(jnp.where(lane == 127, el, er), 1, 1)
    faces = cf[0] + cf[1] + cf[2] + cf[3]
    for l in range(LEVELS):
        put_swapped(kd.at[l], kappa[l])
        kd[l] += faces
    all_p, all_a = range(NP), range(NA)
    place_rows(v0, 0, NP, prow_r.at[0])
    place_cols(phalo, NP, pcol_r.at[0])
    k_pass(v0, v1, 0, all_p, phalo, kd, cf, sums, 1, own=0)
    cols_of(v1, 0, NP, pcol_s.at[1])
    rows_of(v1, 0, NP, prow_s.at[1])
    probe_copies = exchange(prow_s, prow_r, pcol_s, pcol_r, px_s, px_r, 1)

    def arrived(g):
        sources = group_of(g)
        for n, d in enumerate(sources):
            if n:
                station_copy(d, d).wait_recv()
            else:

                @pl.when(g > 0)
                def _():
                    station_copy(d, d).wait_recv()

        return sources

    adj[...] = jnp.zeros((LEVELS * ROWS, COLS), f32)
    scatter_phase(got, adj, arrived, 0, EARLY)
    wait_all(probe_copies)
    place_rows(v1, 0, NP, prow_r.at[1])
    place_cols(phalo, NP, pcol_r.at[1])
    k_pass(v1, v2, 0, all_p, phalo, kd, cf, sums, 2)
    cols_of(v2, 0, NP, pcol_s.at[2])
    rows_of(v2, 0, NP, prow_s.at[2])
    probe_copies = exchange(prow_s, prow_r, pcol_s, pcol_r, px_s, px_r, 2)
    scatter_phase(got, adj, arrived, EARLY, DEV // 8)
    for l in range(LEVELS):
        for h in range(2):
            v0[NP + l, h, 8 : 8 + ROWS, :] = adj[l * ROWS : (l + 1) * ROWS, h * 128 : h * 128 + 128]
    cols_of(v0, NP, NA, acol_s.at[0])
    rows_of(v0, NP, NA, arow_s.at[0])
    copies = exchange(arow_s, arow_r, acol_s, acol_r, ax_s, ax_r, 0)

    wait_all(probe_copies)
    place_rows(v2, 0, NP, prow_r.at[2])
    place_cols(phalo, NP, pcol_r.at[2])
    k_pass(v2, None, 0, range(32), phalo, kd, cf, sums, 3)
    wait_all(copies)
    place_rows(v0, NP, NA, arow_r.at[0])
    place_cols(ahalo, NA, acol_r.at[0])
    k_pass(v0, v1, NP, all_a, ahalo, kd, cf, sums, 1, own=0)
    cols_of(v1, NP, NA, acol_s.at[1])
    rows_of(v1, NP, NA, arow_s.at[1])
    copies = exchange(arow_s, arow_r, acol_s, acol_r, ax_s, ax_r, 1)
    k_pass(v2, None, 0, range(32, NP), phalo, kd, cf, sums, 3)
    wait_all(copies)
    place_rows(v1, NP, NA, arow_r.at[1])
    place_cols(ahalo, NA, acol_r.at[1])
    k_pass(v1, v2, NP, all_a, ahalo, kd, cf, sums, 2)
    cols_of(v2, NP, NA, acol_s.at[2])
    rows_of(v2, NP, NA, arow_s.at[2])
    copies = exchange(arow_s, arow_r, acol_s, acol_r, ax_s, ax_r, 2)
    half = iota((1, 128), 1) < NP
    part = [lane_totals(sums, k, 0, NP) for k in range(4)]
    tot[me, 0:1, :] = jnp.where(half, part[0], pltpu.roll(part[1], NP, 1))
    tot[me, 1:2, :] = jnp.where(half, part[2], pltpu.roll(part[3], NP, 1))
    tot[me, 3:4, :] = jnp.zeros((1, 128), f32)
    wait_all(copies)
    place_rows(v2, NP, NA, arow_r.at[2])
    place_cols(ahalo, NA, acol_r.at[2])
    k_pass(v2, None, NP, all_a, ahalo, kd, cf, sums, 3)
    row = jnp.zeros((1, 128), f32)
    for k in range(4):
        row = row + pltpu.roll(lane_totals(sums, k, NP, NA), NA * k, 1)
    tot[me, 2:3, :] = row

    to_all(total_copy, far_first=True)
    others = pltpu.make_async_remote_copy(
        src_ref=send.at[pl.ds(0, DEV - 1)], dst_ref=got.at[pl.ds(0, DEV - 1)], send_sem=a2a_s, recv_sem=tot_r,
        device_id=lon_peers[0], device_id_type=MESH,
    )
    others.wait_send()
    others = pltpu.make_async_remote_copy(
        src_ref=tot.at[pl.ds(0, DEV - 1)], dst_ref=tot.at[pl.ds(0, DEV - 1)], send_sem=tot_s, recv_sem=tot_r,
        device_id=lon_peers[0], device_id_type=MESH,
    )
    others.wait()
    total = jnp.sum(tot[...], axis=0)
    pt, at = total[0:2], total[2:3]

    is_probe = iota((1, 128), 1) < NP
    ps = [pt[0:1], pltpu.roll(pt[0:1], NP, 1), pt[1:2], pltpu.roll(pt[1:2], NP, 1)]
    s0, s1, s2, s3 = [
        jnp.where(is_probe, ps[k], pltpu.roll(at, (NP - NA * k) % 128, 1)) for k in range(4)
    ]
    alpha = jnp.where(s1 > 0.0, s0 / s1, 0.0)
    next_rr = jnp.maximum(alpha * alpha * s2 - s0, 0.0)
    beta = jnp.where(s0 > 0.0, next_rr / s0, 0.0)
    grow = 1.0 + beta
    denom = grow * grow * s1 - 2.0 * grow * alpha * s2 + alpha * alpha * s3
    step = jnp.where(denom > 0.0, next_rr / denom, 0.0)
    step = jnp.minimum(jnp.maximum(step, STEP_MIN), STEP_MAX)
    scale_b, scale_q = alpha + step * grow, -alpha * step
    spot = iota((NF, 128), 1) == iota((NF, 128), 0)
    for k, scale in enumerate((scale_b, scale_q)):
        column = jnp.sum(jnp.where(spot, scale, 0.0), axis=1, keepdims=True)
        scale_out[k] = jnp.broadcast_to(column, (NF, 128))


def final_kernel(v0, v2, scale, out, block, sem):
    def copy(s, h):
        return pltpu.make_async_copy(block.at[s, :, h], out.at[s, :, :, pl.ds(h * 128, 128)], sem.at[s, h])

    def system(s, _):
        for h in range(2):
            for l in range(LEVELS):
                f = s * LEVELS + l
                sb, sq = scale[0, pl.ds(f, 1), :], scale[1, pl.ds(f, 1), :]
                for t in range(8):
                    at = pl.ds(8 + 8 * t, 8)
                    block[s, l, h, pl.ds(t, 8, stride=8), :] = sb * v0[f, h, at, :] + sq * v2[f, h, at, :]
            copy(s, h).start()
        return 0

    def wait(s, _):
        for h in range(2):
            copy(s, h).wait()
        return 0

    lax.fori_loop(0, 9, system, 0)
    lax.fori_loop(0, 9, wait, 0)


def local(probes, kappa, cond_lat, cond_lon, inno, weight, dest, cell):
    vmem = pl.BlockSpec(memory_space=pltpu.VMEM)
    hbm = pl.BlockSpec(memory_space=pltpu.HBM)
    reg, dma = pltpu.SemaphoreType.REGULAR, pltpu.SemaphoreType.DMA
    probes = probes.reshape(NP, ROWS, COLS)
    weight, cell, dest = weight.reshape(64, 128), cell.reshape(64, 128), dest.reshape(1, HELD)
    args = (probes, kappa, cond_lat, cond_lon, inno, weight, dest, cell)
    buf = lambda *shape: pltpu.VMEM(shape, f32)
    v0, v2, scale = pl.pallas_call(
        main_kernel,
        out_shape=[
            pltpu.VMEM((NF, 2, PAD, 128), f32),
            pltpu.VMEM((NF, 2, PAD, 128), f32),
            pltpu.VMEM((2, NF, 128), f32),
        ],
        in_specs=[hbm] * 8,
        out_specs=[vmem] * 3,
        scratch_shapes=[
            buf(NF, 2, PAD, 128),
            buf(LEVELS * ROWS, COLS), buf(576, 256), buf(1, HELD), buf(DEV, 128),
            buf(DEV, 9, 128), buf(DEV, 9, 128), buf(LEVELS, 2, ROWS, 128), buf(4, 2, ROWS, 128), buf(4, NF, 8, 128),
            buf(3, 2, NF, COLS), buf(3, 2, NF, COLS), buf(3, 2, ROWS, 128), buf(3, 2, ROWS, 128),
            buf(3, 2, NA, COLS), buf(3, 2, NA, COLS), buf(3, 2, ROWS, 128), buf(3, 2, ROWS, 128),
            buf(DEV, 4, 128), buf(NP, ROWS, 128), buf(NA, ROWS, 128),
            reg, dma, dma((DEV,)), dma((3, 4)), dma((3, 4)), dma((3, 4)), dma((3, 4)), dma, dma,
            *[pltpu.VMEM(a.shape, a.dtype) for a in args],
            dma((8,)),
        ],
        compiler_params=pltpu.CompilerParams(
            collective_id=0, has_side_effects=True, vmem_limit_bytes=36 * 2**20
        ),
        name="main",
    )(*[pltpu.with_memory_space_constraint(a, pltpu.HBM) for a in args])
    out = pl.pallas_call(
        final_kernel,
        out_shape=jax.ShapeDtypeStruct((9, LEVELS, ROWS, COLS), f32),
        in_specs=[vmem] * 3,
        out_specs=hbm,
        scratch_shapes=[buf(9, LEVELS, 2, ROWS, 128), dma((9, 2))],
        compiler_params=pltpu.CompilerParams(vmem_limit_bytes=12 * 2**20),
        name="final",
    )(v0, v2, scale)
    return out


def solution(mesh):
    placed = (
        P(None, None, "lat", "lon"),
        P(None, "lat", "lon"),
        P("lat", "lon"),
        P("lat", "lon"),
        P(None, ("lat", "lon")),
        P(("lat", "lon")),
        P(("lat", "lon"), None),
        P(("lat", "lon")),
    )
    return jax.shard_map(
        local, mesh=mesh, in_specs=placed, out_specs=P(None, None, "lat", "lon"), check_vma=False
    )
```
